256 devices in a mesh: dp: 4 (over z_hi), graph: 64 (over y, z_lo, x, core).
Axes of the slice: x: 4, y: 4, z: 8 (z_hi: 4, z_lo: 2; z = z_hi * 2 + z_lo), core: 2. Of those that a mesh axis runs over, the one named last changes fastest.
Arguments:
- inputs: bfloat16 [4, 32768, 256], P('dp', 'graph')
- gain: float32 [256], replicated, may hold values from 0.25 to 1.75
- w_query: bfloat16 [256, 256], replicated
- w_key: bfloat16 [256, 256], replicated
- w_value: bfloat16 [256, 256], replicated, may hold values from -0.375 to 0.375
- w_out: bfloat16 [256, 256], replicated, may hold values from -0.375 to 0.375
- block_slots: int32 [32768], P('graph'), may hold values from 0 to 32767, as said below
- matchings: int32 [4, 128], replicated, may hold values from 0 to 127, as said below
- cotangent: bfloat16 [4, 32768, 256], P('dp', 'graph'), may hold values from -6 to 6
Outputs:
- update: bfloat16 [4, 32768, 256], P('dp', 'graph')
- grad_inputs: bfloat16 [4, 32768, 256], P('dp', 'graph')
- grad_query: float32 [256, 256], replicated
- grad_key: float32 [256, 256], replicated
- grad_value: float32 [256, 256], replicated
- grad_out: float32 [256, 256], replicated
- grad_gain: float32 [256], replicated
The draws below stay inside these ranges and needn't reach their ends.
Inputs may be any that keep to these rules, and one draw needn't show every extreme that they name: `block_slots`: each graph index's 2 * 256 slots hold a permutation of that index's own sensors. `matchings`: each row is an involution of the blocks without fixed points. Block b lives on graph index b // 2; in matching r the partner of every block on index i lives on index i XOR 2 ** ((r * log2(64)) // 4).
All inputs are finite; a program needn't handle non-finite values.
Results may differ from the reference program's by a relative error of at most 0.02.
The reference program's roundings to bfloat16 on the way count: a program that leaves them out, or rounds other values in their place, can miss the bound.
Values may be sent and summed in bfloat16 or wider, within the bound.
A program may use at most 64 MiB of HBM per device.

```python
import math
import jax
import jax.numpy as jnp
from jax import lax

D = 256
HEADS = 8
SB = 256
BLK_DEV = 2
ROUNDS = 4
WIN_DEV = 1
BLOCKS = 128
SENSORS = 32768
WINDOWS = 4
N_DP = 4
N_GRAPH = 64


def projection_draw(key):
    return jnp.clip(jax.random.normal(key, (D, D), jnp.float32), -6.0, 6.0) * (1.8 / math.sqrt(D))


def draw_w_query(key, part):
    key = jax.random.fold_in(key, 5)
    return projection_draw(key).astype(jnp.bfloat16)


def draw_w_key(key, part):
    key = jax.random.fold_in(key, 9)
    return projection_draw(key).astype(jnp.bfloat16)


def draw_inputs(key, part):
    key = jax.random.fold_in(key, 11)
    noise_key = jax.random.fold_in(key, 0)
    shape = (WIN_DEV * N_DP, BLK_DEV * N_GRAPH * SB, D)
    return jnp.clip(jax.random.normal(noise_key, shape, jnp.float32), -6.0, 6.0).astype(jnp.bfloat16)


def draw_block_slots(key, part):
    key = jax.random.fold_in(key, 3)
    per_device = BLK_DEV * SB
    subkeys = jax.random.split(key, N_GRAPH)
    orders = jax.vmap(lambda subkey: jax.random.permutation(subkey, per_device))(subkeys).astype(jnp.int32)
    offsets = jnp.arange(N_GRAPH, dtype=jnp.int32)[:, None] * per_device
    return (orders + offsets).reshape(-1).astype(jnp.int32)


def draw_matchings(key, part):
    key = jax.random.fold_in(key, 7)
    nbits = N_GRAPH.bit_length() - 1
    devices = jnp.arange(N_GRAPH, dtype=jnp.int32)
    stacked = []
    for turn in range(ROUNDS):
        bit_pos = turn * nbits // ROUNDS
        subkeys = jax.random.split(jax.random.fold_in(key, turn), N_GRAPH)
        orders = jax.vmap(lambda subkey: jax.random.permutation(subkey, BLK_DEV))(subkeys).astype(jnp.int32)
        inverse = jnp.argsort(orders, axis=1).astype(jnp.int32)
        partner = jnp.bitwise_xor(devices, 1 << bit_pos)
        lower = jnp.bitwise_and(devices, 1 << bit_pos) == 0
        local_map = jnp.where(lower[:, None], orders, inverse[partner])
        stacked.append((partner[:, None] * BLK_DEV + local_map).reshape(-1))
    return jnp.stack(stacked).astype(jnp.int32)


def levels(key, shape, cuts, least, high):
    def one(position, parts):
        draws = jax.random.uniform(jax.random.fold_in(jax.random.fold_in(key, 6), position), (parts,), jnp.float32, least / len(cuts), high / len(cuts))
        return jnp.repeat(jnp.exp(draws), shape[position] // parts).reshape((-1,) + (1,) * (len(shape) - position - 1))

    factor_of = one(*cuts[0])
    for cut in cuts[1:]:
        factor_of = factor_of * one(*cut)
    return factor_of


def centred(rng, shape, spread, limit, pieces=(), held_as=jnp.bfloat16):
    values = spread * jax.random.normal(rng, shape, jnp.float32)
    if pieces:
        values = values * levels(rng, shape, pieces, -0.22, 0.18)
    return jnp.clip(values, -limit, limit).astype(held_as)


def setup_inputs(seed: int = 0) -> dict:
    splits = jax.random.split(jax.random.key(seed), 10)
    inputs = draw_inputs(jax.random.fold_in(splits[9], 71), 0)
    gain = jnp.clip(1.0 + 0.15 * jax.random.normal(splits[1], (D,), jnp.float32), 0.25, 1.75)
    w_query = draw_w_query(jax.random.fold_in(splits[9], 71), 0)
    w_key = draw_w_key(jax.random.fold_in(splits[9], 71), 0)
    w_value = centred(splits[4], (D, D), D ** -0.5, 0.375)
    w_out = centred(splits[5], (D, D), D ** -0.5, 0.375)
    block_slots = draw_block_slots(jax.random.fold_in(splits[9], 71), 0)
    matchings = draw_matchings(jax.random.fold_in(splits[9], 71), 0)
    cotangent = centred(splits[8], (WINDOWS, SENSORS, D), 1.0, 6.0, ((0, 4), (1, 64)))
    return {"inputs": inputs, "gain": gain, "w_query": w_query, "w_key": w_key, "w_value": w_value, "w_out": w_out, "block_slots": block_slots, "matchings": matchings, "cotangent": cotangent}


epsilon = 1e-06

def attend_block(query_blk, key_blk, value_blk, score_scale):
    scores = jnp.einsum('wqhe,wkhe->whqk', query_blk.astype(jnp.float32), key_blk.astype(jnp.float32)) * score_scale
    row_max = lax.optimization_barrier(jnp.max(scores, axis=-1, keepdims=True))
    expo = jnp.exp(scores - row_max)
    row_sum = lax.optimization_barrier(jnp.sum(expo, axis=-1, keepdims=True))
    probs = expo / row_sum
    weights = probs.astype(jnp.bfloat16)
    attended = jnp.einsum('whqk,wkhe->wqhe', weights.astype(jnp.float32), value_blk.astype(jnp.float32)).astype(jnp.bfloat16)
    return (attended, probs, weights)

def reference(inputs, gain, w_query, w_key, w_value, w_out, block_slots, matchings, cotangent):
    windows = inputs.shape[0]
    head_dim = D // HEADS
    score_scale = head_dim ** (-0.5)
    slotted = jnp.take(inputs, block_slots, axis=1)
    slot_f = slotted.astype(jnp.float32)
    inv_rms = lax.rsqrt(lax.optimization_barrier(jnp.mean(slot_f * slot_f, axis=-1, keepdims=True)) + epsilon)
    normed = (slot_f * inv_rms * gain).astype(jnp.bfloat16)
    norm_rows = normed.reshape(-1, D)

    def project(weight):
        out = jnp.dot(norm_rows, weight, preferred_element_type=jnp.float32).astype(jnp.bfloat16)
        return out.reshape(windows, BLOCKS, SB, HEADS, head_dim)
    queries = project(w_query)
    keys = project(w_key)
    values = project(w_value)
    key_sets = jnp.concatenate([jnp.arange(BLOCKS, dtype=jnp.int32)[None], matchings.astype(jnp.int32)], axis=0).T

    def gather_set(array, members):
        return jnp.take(array, members, axis=1).reshape(windows, (ROUNDS + 1) * SB, HEADS, head_dim)

    def forward_block(block):
        members = key_sets[block]
        return attend_block(queries[:, block], gather_set(keys, members), gather_set(values, members), score_scale)[0]
    attended = lax.map(forward_block, jnp.arange(BLOCKS, dtype=jnp.int32))
    att_rows = jnp.transpose(attended, (1, 0, 2, 3, 4)).reshape(-1, D)
    update_rows = jnp.dot(att_rows, w_out, preferred_element_type=jnp.float32).astype(jnp.bfloat16)
    update = jnp.zeros_like(inputs).at[:, block_slots].set(update_rows.reshape(windows, SENSORS, D))
    cot_rows = jnp.take(cotangent, block_slots, axis=1).reshape(-1, D)
    grad_out = jnp.dot(att_rows.T, cot_rows, preferred_element_type=jnp.float32)
    attended_grad = jnp.dot(cot_rows, w_out.T, preferred_element_type=jnp.float32).astype(jnp.bfloat16)
    attended_grad = attended_grad.reshape(windows, BLOCKS, SB, HEADS, head_dim)

    def backward_block(carry, block):
        key_acc, value_acc = carry
        members = key_sets[block]
        key_blk = gather_set(keys, members)
        value_blk = gather_set(values, members)
        query_blk = queries[:, block]
        grad_blk = attended_grad[:, block]
        unused, probs, weights = attend_block(query_blk, key_blk, value_blk, score_scale)
        prob_grad = jnp.einsum('wqhe,wkhe->whqk', grad_blk.astype(jnp.float32), value_blk.astype(jnp.float32))
        row_dot = lax.optimization_barrier(jnp.sum(prob_grad * probs, axis=-1, keepdims=True))
        score_grad = (probs * (prob_grad - row_dot)).astype(jnp.bfloat16)
        value_part = jnp.einsum('whqk,wqhe->wkhe', weights.astype(jnp.float32), grad_blk.astype(jnp.float32))
        query_part = jnp.einsum('whqk,wkhe->wqhe', score_grad.astype(jnp.float32), key_blk.astype(jnp.float32)) * score_scale
        key_part = jnp.einsum('whqk,wqhe->wkhe', score_grad.astype(jnp.float32), query_blk.astype(jnp.float32)) * score_scale
        key_part = key_part.reshape(windows, ROUNDS + 1, SB, HEADS, head_dim)
        value_part = value_part.reshape(windows, ROUNDS + 1, SB, HEADS, head_dim)
        for member in range(ROUNDS + 1):
            key_acc = key_acc.at[:, members[member]].add(key_part[:, member])
            value_acc = value_acc.at[:, members[member]].add(value_part[:, member])
        return ((key_acc, value_acc), query_part)
    zeros = jnp.zeros((windows, BLOCKS, SB, HEADS, head_dim), jnp.float32)
    (key_acc, value_acc), query_parts = lax.scan(backward_block, (zeros, zeros), jnp.arange(BLOCKS, dtype=jnp.int32))
    query_grad = jnp.transpose(query_parts, (1, 0, 2, 3, 4)).reshape(-1, D).astype(jnp.bfloat16)
    key_grad = key_acc.reshape(-1, D).astype(jnp.bfloat16)
    value_grad = value_acc.reshape(-1, D).astype(jnp.bfloat16)
    grad_query = jnp.dot(norm_rows.T, query_grad, preferred_element_type=jnp.float32)
    grad_key = jnp.dot(norm_rows.T, key_grad, preferred_element_type=jnp.float32)
    grad_value = jnp.dot(norm_rows.T, value_grad, preferred_element_type=jnp.float32)
    normed_grad = jnp.dot(query_grad, w_query.T, preferred_element_type=jnp.float32)
    normed_grad = normed_grad + jnp.dot(key_grad, w_key.T, preferred_element_type=jnp.float32)
    normed_grad = normed_grad + jnp.dot(value_grad, w_value.T, preferred_element_type=jnp.float32)
    normed_grad = normed_grad.reshape(windows, SENSORS, D)
    grad_gain = lax.optimization_barrier(jnp.sum(normed_grad * slot_f * inv_rms, axis=(0, 1)))
    scaled = normed_grad * gain
    slot_grad = inv_rms * scaled - slot_f * (inv_rms * inv_rms * inv_rms) * lax.optimization_barrier(jnp.mean(slot_f * scaled, axis=-1, keepdims=True))
    grad_inputs = jnp.zeros_like(inputs).at[:, block_slots].set(slot_grad.astype(jnp.bfloat16))
    return (update, grad_inputs, grad_query, grad_key, grad_value, grad_out, grad_gain)
```

```python
import functools

import jax
import jax.numpy as jnp
from jax import lax
from jax.experimental import pallas as pl
from jax.experimental.pallas import tpu as pltpu
from jax.sharding import PartitionSpec as P

MESH = pl.DeviceIdType.MESH
HEADS = 8
SPAN = 256
WIDTH = 256
HEAD = 32
HALF = 128
GROUP_HEADS = 4
KEYS = 1280
CHUNKS = 5
ROUNDS = 4
ROWS = 512
NX = 8
NY = 8
ND = 4
EPS = 1e-06
LOG2E = 1.4426950408889634
SCALE = HEAD ** (-0.5)

f32 = jnp.float32
bf16 = jnp.bfloat16


def dot(a, b):
    return jnp.dot(a, b, preferred_element_type=f32)


def dot_nt(a, b):
    return lax.dot_general(a, b, (((1,), (1,)), ((), ())), preferred_element_type=f32)


def flipped(value, mask):
    out = value
    bit = 1
    while bit <= mask:
        if mask & bit:
            out = out + bit - 2 * bit * lax.rem(lax.div(value, bit), 2)
        bit *= 2
    return out


def fold(array, op):
    return op(array.reshape(array.shape[0] // 8, 8, array.shape[1]), axis=0)


def kernel(
    bits,
    x_ref, gain_ref, wq_ref, wk_ref, wv_ref, wo_ref, slot_ref, match_ref, cot_ref,
    upd_ref, ginp_ref, gq_ref, gk_ref, gv_ref, go_ref, gg_ref,
    oht, slot_f, inv_s, normed, nf0, nf1, nf2, nf3, normed_t,
    keys, vals, keys_t, vals_t, cots, qm, gm,
    att_t, dq_t, dkv, exps, ebuf, dsbuf, qpm, gpm,
    rd00, rd01, rd02, rd03, rd10, rd11, rd12, rd13,
    gf, gw, r1, s2, r2, s3, r3, a2, a1,
    ns_send, ns_recv, ds_send, ds_recv,
    s1_send, s1_recv, s2_send, s2_recv, s3_send, s3_recv,
    t2_send, t2_recv, t1_send, t1_recv,
):
    gi = lax.axis_index("graph")
    dp = lax.axis_index("dp")
    low = lax.rem(gi, NX)
    high = lax.div(gi, NX)
    far = (nf0, nf1, nf2, nf3)
    got = ((rd00, rd01, rd02, rd03), (rd10, rd11, rd12, rd13))
    partners = [flipped(gi, 1 << bit) for bit in bits]
    x_peer = [flipped(gi, d) for d in range(1, NX)]
    y_peer = [flipped(gi, d * NX) for d in range(1, NY)]
    d_peer = [flipped(dp, d) for d in range(1, ND)]

    barrier = pltpu.get_barrier_semaphore()
    for peer in x_peer + y_peer:
        pl.semaphore_signal(barrier, inc=1, device_id=(dp, peer), device_id_type=MESH)
    for peer in d_peer:
        pl.semaphore_signal(barrier, inc=1, device_id=(peer, gi), device_id_type=MESH)

    hot_t = (
        lax.broadcasted_iota(jnp.int32, (ROWS, ROWS), 0) == slot_ref[...] - gi * ROWS
    ).astype(f32).astype(bf16)
    oht[...] = hot_t
    hot = hot_t.T
    sx = dot(hot, x_ref[...])
    slot_f[...] = sx
    inv = lax.rsqrt(jnp.mean(sx * sx, axis=-1, keepdims=True) + EPS)
    inv_s[...] = inv
    gain = gain_ref[...]
    nrm = (sx * inv * gain).astype(bf16)
    for b in range(2):
        normed[b] = nrm[b * SPAN : (b + 1) * SPAN]

    pl.semaphore_wait(barrier, NX + NY + ND - 3)
    sends = []
    for r in range(ROUNDS):
        copy = pltpu.make_async_remote_copy(
            src_ref=normed, dst_ref=far[r], send_sem=ns_send.at[r], recv_sem=ns_recv.at[r],
            device_id=(dp, partners[r]), device_id_type=MESH,
        )
        copy.start()
        sends.append(copy)
    far_copies = list(sends)

    cs = dot(hot, cot_ref[...]).astype(bf16)
    cots[...] = cs
    wk_t = wk_ref[...].T
    wv_t = wv_ref[...].T
    q_t = dot_nt(wq_ref[...].T, nrm).astype(bf16)
    g_t = dot_nt(wo_ref[...], cs).astype(bf16)
    head_of = lax.broadcasted_iota(jnp.int32, (HALF, SPAN), 0) // HEAD
    for g in range(2):
        for b in range(2):
            qs = q_t[g * HALF : (g + 1) * HALF, b * SPAN : (b + 1) * SPAN]
            gs = g_t[g * HALF : (g + 1) * HALF, b * SPAN : (b + 1) * SPAN]
            for hh in range(GROUP_HEADS):
                qm[b, g, hh] = jnp.where(head_of == hh, qs, jnp.zeros_like(qs))
                gm[b, g, hh] = jnp.where(head_of == hh, gs, jnp.zeros_like(gs))

    def add_keys(b, c, rows):
        span = pl.ds(c * SPAN, SPAN)
        k = dot(rows, wk_ref[...]).astype(bf16)
        v = dot(rows, wv_ref[...]).astype(bf16)
        kt = dot_nt(wk_t, rows).astype(bf16)
        vt = dot_nt(wv_t, rows).astype(bf16)
        normed_t[b, :, span] = rows.T
        for g in range(2):
            half = slice(g * HALF, (g + 1) * HALF)
            keys[b, g, span, :] = k[:, half]
            vals[b, g, span, :] = v[:, half]
            keys_t[b, g, :, span] = kt[half]
            vals_t[b, g, :, span] = vt[half]

    pairs = [
        [lax.rem(match_ref[r, 2 * gi + b], 2) for b in range(2)] for r in range(ROUNDS)
    ]
    for b in range(2):
        add_keys(b, 0, normed[b])
    for r in range(ROUNDS):
        far_copies[r].wait_recv()
        for b in range(2):
            add_keys(b, r + 1, far[r][pairs[r][b]])

    def head(b, g, hh):
        slot = hh % 2
        lane = pl.ds(hh * SPAN, SPAN)
        row = pl.ds(hh * HEAD, HEAD)
        query = qm[b, g, hh]
        grad = gm[b, g, hh]
        top = None
        for c in range(CHUNKS):
            span = pl.ds(c * SPAN, SPAN)
            s = dot(keys[b, g, span, :], query)
            exps[slot, span, :] = s
            m = fold(s, jnp.max)
            top = m if top is None else jnp.maximum(top, m)
        top = jnp.max(top, axis=0, keepdims=True) * (SCALE * LOG2E)
        total = None
        o = None
        for c in range(CHUNKS):
            span = pl.ds(c * SPAN, SPAN)
            e = jnp.exp2(exps[slot, span, :] * (SCALE * LOG2E) - top)
            exps[slot, span, :] = e
            t = fold(e, jnp.sum)
            total = t if total is None else total + t
            eb = e.astype(bf16)
            ebuf[span, lane] = eb
            p = dot(vals_t[b, g, row, span], eb)
            o = p if o is None else o + p
        rinv = 1.0 / jnp.sum(total, axis=0, keepdims=True)
        o = o * rinv
        att_t[g, row, pl.ds(b * SPAN, SPAN)] = o.astype(bf16)
        mine = gm[b, g, hh, row, :].astype(f32)
        delta = jnp.sum(mine * o, axis=0, keepdims=True)
        qpm[:, lane] = (query.astype(f32) * (rinv * SCALE)).astype(bf16)
        gpm[:, lane] = (grad.astype(f32) * rinv).astype(bf16)
        dq = None
        for c in range(CHUNKS):
            span = pl.ds(c * SPAN, SPAN)
            dprob = dot(vals[b, g, span, :], grad)
            ds = (exps[slot, span, :] * (dprob - delta)).astype(bf16)
            dsbuf[span, lane] = ds
            p = dot(keys_t[b, g, row, span], ds)
            dq = p if dq is None else dq + p
        dq_t[g, row, pl.ds(b * SPAN, SPAN)] = (dq * (rinv * SCALE)).astype(bf16)

    def attend(b, g, hooks):
        for hh in range(GROUP_HEADS):
            head(b, g, hh)
            if hooks:
                hooks.pop(0)()
        for c in range(CHUNKS):
            span = pl.ds(c * SPAN, SPAN)
            dkv[g, c, 1, b] = dot_nt(ebuf[span, :], gpm[...]).astype(bf16)
            dkv[g, c, 0, b] = dot_nt(dsbuf[span, :], qpm[...]).astype(bf16)

    def weight_grads(g):
        gq = None
        gk = None
        gv = None
        for b in range(2):
            p = dot_nt(normed_t[b, :, 0:SPAN], dq_t[g, :, b * SPAN : (b + 1) * SPAN])
            gq = p if gq is None else gq + p
            for c in range(CHUNKS):
                nt = normed_t[b, :, c * SPAN : (c + 1) * SPAN]
                p = dot(nt, dkv[g, c, 0, b])
                gk = p if gk is None else gk + p
                p = dot(nt, dkv[g, c, 1, b])
                gv = p if gv is None else gv + p
        go = dot(att_t[g], cots[...])
        for at, part in (
            (0, gq), (256, gk), (512, gv), (768, go[:, :HALF]), (896, go[:, HALF:])
        ):
            n = part.shape[0]
            gf[g, at : at + n] = part
            gw[g, at : at + n] = part.astype(bf16)

    grads_far = [[], []]

    def send_grads(g):
        for r in range(ROUNDS):
            copy = pltpu.make_async_remote_copy(
                src_ref=dkv.at[g, r + 1], dst_ref=got[g][r],
                send_sem=ds_send.at[g, r], recv_sem=ds_recv.at[g, r],
                device_id=(dp, partners[r]), device_id_type=MESH,
            )
            copy.start()
            sends.append(copy)
            grads_far[g].append(copy)

    flight = {}

    def start(name, g, copies):
        for copy in copies:
            copy.start()
        sends.extend(copies)
        flight[name, g] = copies

    def arrived(name, g):
        for copy in flight[name, g]:
            copy.wait_recv()

    def remote(src, dst, send, recv, to):
        return pltpu.make_async_remote_copy(
            src_ref=src, dst_ref=dst, send_sem=send, recv_sem=recv,
            device_id=to, device_id_type=MESH,
        )

    def stage1(g):
        start("s1", g, [
            remote(
                gw.at[g, pl.ds(flipped(low, d) * 128, 128)], r1.at[g, d - 1],
                s1_send.at[g, d - 1], s1_recv.at[g, d - 1], (dp, x_peer[d - 1]),
            )
            for d in range(1, NX)
        ])

    def stage2(g):
        arrived("s1", g)
        total = gf[g, pl.ds(low * 128, 128)]
        for d in range(1, NX):
            total = total + r1[g, d - 1].astype(f32)
        s2[g] = total
        start("s2", g, [
            remote(
                s2.at[g, pl.ds(flipped(high, d) * 16, 16)], r2.at[g, d - 1],
                s2_send.at[g, d - 1], s2_recv.at[g, d - 1], (dp, y_peer[d - 1]),
            )
            for d in range(1, NY)
        ])

    def stage3(g):
        arrived("s2", g)
        total = s2[g, pl.ds(high * 16, 16)]
        for d in range(1, NY):
            total = total + r2[g, d - 1]
        s3[g] = total
        start("s3", g, [
            remote(
                s3.at[g], r3.at[g, d - 1],
                s3_send.at[g, d - 1], s3_recv.at[g, d - 1], (d_peer[d - 1], gi),
            )
            for d in range(1, ND)
        ])

    def stage4(g):
        arrived("s3", g)
        mine = pl.ds(high * 16, 16)
        a2[g, mine] = ((s3[g] + r3[g, 0]) + (r3[g, 1] + r3[g, 2])).astype(bf16)
        start("t2", g, [
            remote(
                a2.at[g, mine], a2.at[g, mine],
                t2_send.at[g, d - 1], t2_recv.at[g, d - 1], (dp, y_peer[d - 1]),
            )
            for d in range(1, NY)
        ])

    def stage5(g):
        arrived("t2", g)
        mine = pl.ds(low * 128, 128)
        start("t1", g, [
            remote(
                a2.at[g], a1.at[g, mine],
                t1_send.at[g, d - 1], t1_recv.at[g, d - 1], (dp, x_peer[d - 1]),
            )
            for d in range(1, NX)
        ])
        a1[g, mine] = a2[g]

    def finish(g):
        arrived("t1", g)
        cols = slice(g * HALF, (g + 1) * HALF)
        gq_ref[:, cols] = a1[g, 0:256].astype(f32)
        gk_ref[:, cols] = a1[g, 256:512].astype(f32)
        gv_ref[:, cols] = a1[g, 512:768].astype(f32)
        go_ref[cols, 0:HALF] = a1[g, 768:896].astype(f32)
        go_ref[cols, HALF:WIDTH] = a1[g, 896:1024].astype(f32)

    attend(0, 0, [])
    attend(1, 0, [])
    send_grads(0)
    weight_grads(0)
    stage1(0)
    none = lambda: None
    attend(0, 1, [none, lambda: stage2(0), none, lambda: stage3(0)])
    attend(1, 1, [none, lambda: stage4(0), lambda: stage5(0), lambda: finish(0)])
    weight_grads(1)
    stage1(1)
    send_grads(1)

    att = jnp.concatenate([att_t[0].T, att_t[1].T], axis=1)
    upd = dot(att, wo_ref[...]).astype(bf16)
    upd_ref[...] = dot(oht[...], upd).astype(bf16)
    stage2(1)
    qg = jnp.concatenate([dq_t[0].T, dq_t[1].T], axis=1)
    ng_q = dot_nt(qg, wq_ref[...])
    stage3(1)
    for copy in grads_far[0]:
        copy.wait_recv()
    stage4(1)
    for copy in grads_far[1]:
        copy.wait_recv()
    stage5(1)
    outs = []
    for b in range(2):
        sums = []
        for kv in range(2):
            halves = []
            for g in range(2):
                t = dkv[g, 0, kv, b].astype(f32)
                for r in range(ROUNDS):
                    t = t + got[g][r][kv, pairs[r][b]].astype(f32)
                halves.append(t.astype(bf16))
            sums.append(jnp.concatenate(halves, axis=1))
        rows = slice(b * SPAN, (b + 1) * SPAN)
        ng = ng_q[rows] + dot_nt(sums[0], wk_ref[...]) + dot_nt(sums[1], wv_ref[...])
        scaled = ng * gain
        x = slot_f[rows]
        iv = inv_s[rows]
        mean = jnp.mean(x * scaled, axis=-1, keepdims=True)
        outs.append((iv * scaled - x * (iv * iv * iv) * mean).astype(bf16))
    ginp_ref[...] = dot(oht[...], jnp.concatenate(outs, axis=0)).astype(bf16)
    finish(1)
    prod = (
        gq_ref[...] * wq_ref[...].astype(f32)
        + gk_ref[...] * wk_ref[...].astype(f32)
        + gv_ref[...] * wv_ref[...].astype(f32)
    )
    gg_ref[...] = jnp.sum(prod.T, axis=0, keepdims=True) / gain
    for copy in sends:
        copy.wait_send()


def local(inputs, gain, w_query, w_key, w_value, w_out, block_slots, matchings, cotangent):
    nbits = lax.axis_size("graph").bit_length() - 1
    rounds = matchings.shape[0]
    bits = tuple(turn * nbits // rounds for turn in range(rounds))
    vmem = pl.BlockSpec(memory_space=pltpu.VMEM)
    smem = pl.BlockSpec(memory_space=pltpu.SMEM)
    dma = pltpu.SemaphoreType.DMA
    far = pltpu.VMEM((2, SPAN, WIDTH), bf16)
    got = pltpu.VMEM((2, 2, SPAN, HALF), bf16)
    scratch = [
        pltpu.VMEM((ROWS, ROWS), bf16),
        pltpu.VMEM((ROWS, WIDTH), f32),
        pltpu.VMEM((ROWS, 1), f32),
        far, far, far, far, far,
        pltpu.VMEM((2, WIDTH, KEYS), bf16),
        pltpu.VMEM((2, 2, KEYS, HALF), bf16),
        pltpu.VMEM((2, 2, KEYS, HALF), bf16),
        pltpu.VMEM((2, 2, HALF, KEYS), bf16),
        pltpu.VMEM((2, 2, HALF, KEYS), bf16),
        pltpu.VMEM((ROWS, WIDTH), bf16),
        pltpu.VMEM((2, 2, GROUP_HEADS, HALF, SPAN), bf16),
        pltpu.VMEM((2, 2, GROUP_HEADS, HALF, SPAN), bf16),
        pltpu.VMEM((2, HALF, ROWS), bf16),
        pltpu.VMEM((2, HALF, ROWS), bf16),
        pltpu.VMEM((2, CHUNKS, 2, 2, SPAN, HALF), bf16),
        pltpu.VMEM((2, KEYS, SPAN), f32),
        pltpu.VMEM((KEYS, GROUP_HEADS * SPAN), bf16),
        pltpu.VMEM((KEYS, GROUP_HEADS * SPAN), bf16),
        pltpu.VMEM((HALF, GROUP_HEADS * SPAN), bf16),
        pltpu.VMEM((HALF, GROUP_HEADS * SPAN), bf16),
        got, got, got, got, got, got, got, got,
        pltpu.VMEM((2, 1024, HALF), f32),
        pltpu.VMEM((2, 1024, HALF), bf16),
        pltpu.VMEM((2, NX - 1, 128, HALF), bf16),
        pltpu.VMEM((2, 128, HALF), f32),
        pltpu.VMEM((2, NY - 1, 16, HALF), f32),
        pltpu.VMEM((2, 16, HALF), f32),
        pltpu.VMEM((2, ND - 1, 16, HALF), f32),
        pltpu.VMEM((2, 128, HALF), bf16),
        pltpu.VMEM((2, 1024, HALF), bf16),
        dma((ROUNDS,)), dma((ROUNDS,)), dma((2, ROUNDS)), dma((2, ROUNDS)),
        dma((2, NX - 1)), dma((2, NX - 1)), dma((2, NY - 1)), dma((2, NY - 1)),
        dma((2, ND - 1)), dma((2, ND - 1)),
        dma((2, NY - 1)), dma((2, NY - 1)), dma((2, NX - 1)), dma((2, NX - 1)),
    ]
    square = jax.ShapeDtypeStruct((WIDTH, WIDTH), f32)
    rows = jax.ShapeDtypeStruct((ROWS, WIDTH), bf16)
    update, grad_inputs, gq, gk, gv, go, gg = pl.pallas_call(
        functools.partial(kernel, bits),
        out_shape=(rows, rows, square, square, square, square,
                   jax.ShapeDtypeStruct((1, WIDTH), f32)),
        in_specs=[vmem] * 7 + [smem, vmem],
        out_specs=(vmem,) * 7,
        scratch_shapes=scratch,
        compiler_params=pltpu.CompilerParams(
            collective_id=0, has_side_effects=True, vmem_limit_bytes=56 * 2**20
        ),
    )(
        inputs[0], gain.reshape(1, WIDTH), w_query, w_key, w_value, w_out,
        block_slots.reshape(1, ROWS), matchings, cotangent[0],
    )
    return update[None], grad_inputs[None], gq, gk, gv, go, gg[0]


def solution(mesh):
    placed = (
        P("dp", "graph", None), P(), P(), P(), P(), P(), P("graph"), P(), P("dp", "graph", None),
    )
    return jax.shard_map(
        local,
        mesh=mesh,
        in_specs=placed,
        out_specs=(P("dp", "graph", None), P("dp", "graph", None), P(), P(), P(), P(), P()),
        check_vma=False,
    )
```

```python
import functools

import jax
import jax.numpy as jnp
from jax import lax
from jax.experimental import pallas as pl
from jax.experimental.pallas import tpu as pltpu
from jax.sharding import PartitionSpec as P

MESH = pl.DeviceIdType.MESH
SPAN = 256
WIDTH = 256
HEAD = 32
HALF = 128
QUART = 64
PIECES = 4
KEYS = 1280
CHUNKS = 5
ROUNDS = 4
ROWS = 512
NX = 32
NZ = 8
EPS = 1e-06
LOG2E = 1.4426950408889634
SCALE = HEAD ** (-0.5)
GROUPS = ((0, 1), (2, 3))
EARLY = 2

f32 = jnp.float32
bf16 = jnp.bfloat16


def dot(a, b):
    return jnp.dot(a, b, preferred_element_type=f32)


def dot_nt(a, b):
    return lax.dot_general(a, b, (((1,), (1,)), ((), ())), preferred_element_type=f32)


def flipped(value, mask):
    out = value
    bit = 1
    while bit <= mask:
        if mask & bit:
            out = out + bit - 2 * bit * lax.rem(lax.div(value, bit), 2)
        bit *= 2
    return out


def fold(array, op):
    return op(array.reshape(array.shape[0] // 8, 8, array.shape[1]), axis=0)


def remote(src, dst, send, recv, to):
    return pltpu.make_async_remote_copy(
        src_ref=src, dst_ref=dst, send_sem=send, recv_sem=recv,
        device_id=to, device_id_type=MESH,
    )


def kernel(bits, *refs):
    (
        x_ref, gain_ref, wq_ref, wk_ref, wv_ref, wo_ref, slot_ref, match_ref, cot_ref,
        upd_ref, ginp_ref,
    ) = refs[:11]
    ng = len(GROUPS)
    a1 = refs[11 : 11 + ng]
    refs = refs[11 + ng :]
    (
        oht, slot_f, inv_s, normed, nf0, nf1, nf2, nf3, normed_t,
        keys, vals, keys_t, vals_t, cots_t, wkv, qm, gm,
        att_t, dq_t, dkv, exps, stack, mixer,
    ) = refs[:23]
    got = [refs[23 + 4 * p : 27 + 4 * p] for p in range(PIECES)]
    refs = refs[39:]
    gf, gw, r1, s2, r3 = [refs[ng * k : ng * k + ng] for k in range(5)]
    (
        ns_send, ns_recv, ds_send, ds_recv,
        s1_send, s1_recv, s3_send, s3_recv, t1_send, t1_recv,
    ) = refs[5 * ng :]

    gi = lax.axis_index("graph")
    dp = lax.axis_index("dp")
    spot = lax.rem(gi, 8) + 8 * lax.div(gi, 16)
    far = (nf0, nf1, nf2, nf3)
    partners = [(dp, flipped(gi, 1 << bit)) for bit in bits]
    x_peer = [(dp, flipped(gi, m % 8 + 16 * (m // 8))) for m in range(1, NX)]
    z_peer = [(flipped(dp, m // 2), flipped(gi, 8 * (m % 2))) for m in range(1, NZ)]

    barrier = pltpu.get_barrier_semaphore()
    for peer in x_peer + z_peer:
        pl.semaphore_signal(barrier, inc=1, device_id=peer, device_id_type=MESH)

    hot_t = (
        lax.broadcasted_iota(jnp.int32, (ROWS, ROWS), 0) == slot_ref[...] - gi * ROWS
    ).astype(f32).astype(bf16)
    oht[...] = hot_t
    hot = hot_t.T
    sx = dot(hot, x_ref[...])
    slot_f[...] = sx
    inv = lax.rsqrt(jnp.mean(sx * sx, axis=-1, keepdims=True) + EPS)
    inv_s[...] = inv
    gain = gain_ref[...]
    nrm = (sx * inv * gain).astype(bf16)
    for b in range(2):
        normed[b] = nrm[b * SPAN : (b + 1) * SPAN]

    pl.semaphore_wait(barrier, NX + NZ - 2)
    sends = []
    far_copies = []
    for r in range(ROUNDS):
        far_copies.append(
            remote(normed, far[r], ns_send.at[r], ns_recv.at[r], partners[r])
        )
    for copy in far_copies:
        copy.start()
        sends.append(copy)

    mixer[...] = jnp.zeros_like(mixer)
    cs = dot(hot, cot_ref[...]).astype(bf16)
    cots_t[...] = cs.T
    wk_t = wk_ref[...].T
    wv_t = wv_ref[...].T
    for p in range(PIECES):
        part = slice(p * QUART, (p + 1) * QUART)
        wkv[p * HALF : p * HALF + QUART] = wk_t[part]
        wkv[p * HALF + QUART : (p + 1) * HALF] = wv_t[part]
    q_t = dot_nt(wq_ref[...].T, nrm).astype(bf16)
    g_t = dot_nt(wo_ref[...], cs).astype(bf16)
    head_of = lax.broadcasted_iota(jnp.int32, (HALF, SPAN), 0) // HEAD
    for g in range(2):
        for b in range(2):
            qs = q_t[g * HALF : (g + 1) * HALF, b * SPAN : (b + 1) * SPAN]
            gs = g_t[g * HALF : (g + 1) * HALF, b * SPAN : (b + 1) * SPAN]
            for hh in range(4):
                qm[b, 4 * g + hh] = jnp.where(head_of == hh, qs, jnp.zeros_like(qs))
                gm[b, 4 * g + hh] = jnp.where(head_of == hh, gs, jnp.zeros_like(gs))

    def add_keys(b, c, rows):
        span = pl.ds(c * SPAN, SPAN)
        k = dot(rows, wk_ref[...]).astype(bf16)
        v = dot(rows, wv_ref[...]).astype(bf16)
        for g in range(2):
            half = slice(g * HALF, (g + 1) * HALF)
            keys[b, g, span, :] = k[:, half]
            vals[b, g, span, :] = v[:, half]
        keys_t[b, :, span] = dot_nt(wk_t, rows).astype(bf16)
        vals_t[b, :, span] = dot_nt(wv_t, rows).astype(bf16)
        normed_t[b, :, span] = rows.T

    units = [(p, b, 2 * p + i) for p in range(PIECES) for b in range(2) for i in range(2)]
    top = {}
    total = {}
    out = {}
    scale_of = {}
    shift = {}
    delta = {}
    dq = {}

    def scores(u, c):
        p, b, h = units[u]
        span = pl.ds(c * SPAN, SPAN)
        s = dot(keys[b, p // 2, span, :], qm[b, h])
        exps[u, span, :] = s
        m = fold(s, jnp.max)
        top[u] = m if c == 0 else jnp.maximum(top[u], m)

    def softmax(u, c):
        p, b, h = units[u]
        span = pl.ds(c * SPAN, SPAN)
        if c == 0:
            shift[u] = jnp.max(top[u], axis=0, keepdims=True) * (SCALE * LOG2E)
        e = jnp.exp2(exps[u, span, :] * (SCALE * LOG2E) - shift[u])
        exps[u, span, :] = e
        t = fold(e, jnp.sum)
        total[u] = t if c == 0 else total[u] + t
        eb = e.astype(bf16)
        stack[(u // 2) % 2, span, pl.ds((2 + u % 2) * SPAN, SPAN)] = eb
        o = dot(vals_t[b, pl.ds(h * HEAD, HEAD), span], eb)
        out[u] = o if c == 0 else out[u] + o

    def middle(u):
        p, b, h = units[u]
        i = u % 2
        rinv = 1.0 / jnp.sum(total[u], axis=0, keepdims=True)
        o = out[u] * rinv
        att_t[pl.ds(h * HEAD, HEAD), pl.ds(b * SPAN, SPAN)] = o.astype(bf16)
        row = pl.ds((h % 4) * HEAD, HEAD)
        grad = gm[b, h, row, :].astype(f32)
        query = qm[b, h, row, :].astype(f32)
        delta[u] = jnp.sum(grad * o, axis=0, keepdims=True)
        scale_of[u] = rinv * SCALE
        half = (u // 2) % 2
        mixer[half, pl.ds(i * HEAD, HEAD), pl.ds(i * SPAN, SPAN)] = (
            query * scale_of[u]
        ).astype(bf16)
        mixer[half, pl.ds(QUART + i * HEAD, HEAD), pl.ds((2 + i) * SPAN, SPAN)] = (
            grad * rinv
        ).astype(bf16)

    def score_grad(u, c):
        p, b, h = units[u]
        span = pl.ds(c * SPAN, SPAN)
        dprob = dot(vals[b, p // 2, span, :], gm[b, h])
        ds = (exps[u, span, :] * (dprob - delta[u])).astype(bf16)
        stack[(u // 2) % 2, span, pl.ds((u % 2) * SPAN, SPAN)] = ds
        q = dot(keys_t[b, pl.ds(h * HEAD, HEAD), span], ds)
        dq[u] = q if c == 0 else dq[u] + q

    def close(u):
        p, b, h = units[u]
        dq_t[pl.ds(h * HEAD, HEAD), pl.ds(b * SPAN, SPAN)] = (dq[u] * scale_of[u]).astype(bf16)

    def key_grads(u, c):
        p, b, h = units[u]
        half = (u // 2) % 2
        dkv[p, c, b] = dot_nt(
            stack[half, pl.ds(c * SPAN, SPAN), :], mixer[half]
        ).astype(bf16)

    def weight_grads(k):
        for i, p in enumerate(GROUPS[k]):
            feats = pl.ds(p * QUART, QUART)
            kv = None
            for b in range(2):
                for c in range(CHUNKS):
                    part = dot(normed_t[b, :, c * SPAN : (c + 1) * SPAN], dkv[p, c, b])
                    kv = part if kv is None else kv + part
            gq = dot_nt(normed_t[0, :, 0:SPAN], dq_t[feats, 0:SPAN]) + dot_nt(
                normed_t[1, :, 0:SPAN], dq_t[feats, SPAN:ROWS]
            )
            go = dot_nt(cots_t[...], att_t[feats, :])
            both = jnp.concatenate([gq, go], axis=1)
            at = i * ROWS
            gf[k][at : at + WIDTH] = kv
            gf[k][at + WIDTH : at + ROWS] = both
            gw[k][at : at + WIDTH] = kv.astype(bf16)
            gw[k][at + WIDTH : at + ROWS] = both.astype(bf16)

    grads_far = {}

    def send_grads(p):
        grads_far[p] = [
            remote(
                dkv.at[p, r + 1], got[p][r], ds_send.at[p, r], ds_recv.at[p, r], partners[r]
            )
            for r in range(ROUNDS)
        ]
        for copy in grads_far[p]:
            copy.start()
        sends.extend(grads_far[p])

    flight = {}

    def start(name, k, copies):
        for copy in copies:
            copy.start()
        sends.extend(copies)
        flight[name, k] = copies

    def arrived(name, k):
        for copy in flight[name, k]:
            copy.wait_recv()

    def spread(k):
        n = len(GROUPS[k]) * ROWS // NX
        start("s1", k, [
            remote(
                gw[k].at[pl.ds(flipped(spot, m) * n, n)], r1[k].at[m - 1],
                s1_send.at[k, m - 1], s1_recv.at[k, m - 1], x_peer[m - 1],
            )
            for m in range(1, NX)
        ])

    def across(k):
        n = len(GROUPS[k]) * ROWS // NX
        arrived("s1", k)
        acc = gf[k][pl.ds(spot * n, n)]
        for m in range(1, NX):
            acc = acc + r1[k][m - 1].astype(f32)
        s2[k][...] = acc
        start("s3", k, [
            remote(
                s2[k], r3[k].at[m - 1],
                s3_send.at[k, m - 1], s3_recv.at[k, m - 1], z_peer[m - 1],
            )
            for m in range(1, NZ)
        ])

    def gather(k):
        n = len(GROUPS[k]) * ROWS // NX
        arrived("s3", k)
        mine = pl.ds(spot * n, n)
        level = [s2[k][...]] + [r3[k][m - 1] for m in range(1, NZ)]
        while len(level) > 1:
            level = [level[j] + level[j + 1] for j in range(0, len(level), 2)]
        a1[k][mine] = level[0].astype(bf16)
        start("t1", k, [
            remote(
                a1[k].at[mine], a1[k].at[mine],
                t1_send.at[k, m - 1], t1_recv.at[k, m - 1], x_peer[m - 1],
            )
            for m in range(1, NX)
        ])

    for b in range(2):
        add_keys(b, 0, normed[b])
    for u in range(len(units)):
        for c in range(min(EARLY, 1)):
            scores(u, c)
    pairs = [
        [lax.rem(match_ref[r, 2 * gi + b], 2) for b in range(2)] for r in range(ROUNDS)
    ]
    for r in range(ROUNDS):
        far_copies[r].wait_recv()
        for b in range(2):
            add_keys(b, r + 1, far[r][pairs[r][b]])
        if r + 1 < EARLY:
            for u in range(len(units)):
                scores(u, r + 1)

    hooks = {
        4: [lambda: send_grads(0)],
        8: [lambda: send_grads(1), lambda: weight_grads(0), lambda: spread(0)],
        12: [lambda: send_grads(2), lambda: across(0)],
        15: [lambda: gather(0)],
    }
    last = len(units) - 1
    for c in range(EARLY, CHUNKS):
        scores(0, c)
    for u in range(len(units)):
        for c in range(CHUNKS):
            if u < last and c >= EARLY:
                scores(u + 1, c)
            softmax(u, c)
        middle(u)
        for c in range(CHUNKS):
            score_grad(u, c)
            if u % 2 == 0 and u >= 2:
                key_grads(u - 1, c)
        close(u)
        for hook in hooks.get(u, []):
            hook()
    for c in range(CHUNKS):
        key_grads(last, c)
    weight_grads(1)
    spread(1)
    send_grads(3)

    upd = dot(att_t[...].T, wo_ref[...]).astype(bf16)
    upd_ref[...] = dot(oht[...], upd).astype(bf16)
    ng_q = dot_nt(dq_t[...].T, wq_ref[...])
    across(1)

    def key_total(p, b):
        t = dkv[p, 0, b].astype(f32)
        for r in range(ROUNDS):
            t = t + got[p][r][pairs[r][b]].astype(f32)
        return t.astype(bf16)

    for p in range(PIECES):
        for copy in grads_far[p]:
            copy.wait_recv()
    outs = []
    for b in range(2):
        sums = jnp.concatenate([key_total(p, b) for p in range(PIECES)], axis=1)
        rows = slice(b * SPAN, (b + 1) * SPAN)
        ngrad = ng_q[rows] + dot(sums, wkv[...])
        scaled = ngrad * gain
        x = slot_f[rows]
        iv = inv_s[rows]
        mean = jnp.mean(x * scaled, axis=-1, keepdims=True)
        outs.append((iv * scaled - x * (iv * iv * iv) * mean).astype(bf16))
    ginp_ref[...] = dot(oht[...], jnp.concatenate(outs, axis=0)).astype(bf16)
    gather(1)
    for k in range(ng):
        arrived("t1", k)
    for copy in sends:
        copy.wait_send()


def finish(*refs):
    ng = len(GROUPS)
    upd, ginp = refs[:2]
    sums = refs[2 : 2 + ng]
    gain_ref, wq_ref, wk_ref, wv_ref = refs[2 + ng : 6 + ng]
    upd_ref, ginp_ref, gq_ref, gk_ref, gv_ref, go_ref, gg_ref = refs[6 + ng :]
    upd_ref[...] = upd[...]
    ginp_ref[...] = ginp[...]
    kv = {}
    qo = {}
    for k, group in enumerate(GROUPS):
        for i, p in enumerate(group):
            at = i * ROWS
            kv[p] = sums[k][at : at + WIDTH].astype(f32)
            qo[p] = sums[k][at + WIDTH : at + ROWS].astype(f32)
    first, second = slice(0, QUART), slice(QUART, HALF)

    def joined(parts, half):
        return jnp.concatenate([parts[p][:, half] for p in range(PIECES)], axis=1)

    gk, gv, gq = joined(kv, first), joined(kv, second), joined(qo, first)
    gq_ref[...] = gq
    gk_ref[...] = gk
    gv_ref[...] = gv
    go_ref[...] = joined(qo, second).T
    prod = (
        gq * wq_ref[...].astype(f32) + gk * wk_ref[...].astype(f32)
        + gv * wv_ref[...].astype(f32)
    )
    gg_ref[...] = jnp.sum(prod.T, axis=0, keepdims=True) / gain_ref[...]


def local(inputs, gain, w_query, w_key, w_value, w_out, block_slots, matchings, cotangent):
    nbits = lax.axis_size("graph").bit_length() - 1
    rounds = matchings.shape[0]
    bits = tuple(turn * nbits // rounds for turn in range(rounds))
    vmem = pl.BlockSpec(memory_space=pltpu.VMEM)
    smem = pl.BlockSpec(memory_space=pltpu.SMEM)
    dma = pltpu.SemaphoreType.DMA
    ng = len(GROUPS)
    size = [len(group) * ROWS for group in GROUPS]
    far = pltpu.VMEM((2, SPAN, WIDTH), bf16)
    got = pltpu.VMEM((2, SPAN, HALF), bf16)
    units = 4 * PIECES
    scratch = [
        pltpu.VMEM((ROWS, ROWS), bf16),
        pltpu.VMEM((ROWS, WIDTH), f32),
        pltpu.VMEM((ROWS, 1), f32),
        far, far, far, far, far,
        pltpu.VMEM((2, WIDTH, KEYS), bf16),
        pltpu.VMEM((2, 2, KEYS, HALF), bf16),
        pltpu.VMEM((2, 2, KEYS, HALF), bf16),
        pltpu.VMEM((2, WIDTH, KEYS), bf16),
        pltpu.VMEM((2, WIDTH, KEYS), bf16),
        pltpu.VMEM((WIDTH, ROWS), bf16),
        pltpu.VMEM((ROWS, WIDTH), bf16),
        pltpu.VMEM((2, 8, HALF, SPAN), bf16),
        pltpu.VMEM((2, 8, HALF, SPAN), bf16),
        pltpu.VMEM((WIDTH, ROWS), bf16),
        pltpu.VMEM((WIDTH, ROWS), bf16),
        pltpu.VMEM((PIECES, CHUNKS, 2, SPAN, HALF), bf16),
        pltpu.VMEM((units, KEYS, SPAN), f32),
        pltpu.VMEM((2, KEYS, 4 * SPAN), bf16),
        pltpu.VMEM((2, HALF, 4 * SPAN), bf16),
    ]
    scratch += [got] * (PIECES * ROUNDS)
    scratch += [pltpu.VMEM((n, HALF), f32) for n in size]
    scratch += [pltpu.VMEM((n, HALF), bf16) for n in size]
    scratch += [pltpu.VMEM((NX - 1, n // NX, HALF), bf16) for n in size]
    scratch += [pltpu.VMEM((n // NX, HALF), f32) for n in size]
    scratch += [pltpu.VMEM((NZ - 1, n // NX, HALF), f32) for n in size]
    scratch += [
        dma((ROUNDS,)), dma((ROUNDS,)), dma((PIECES, ROUNDS)), dma((PIECES, ROUNDS)),
        dma((ng, NX - 1)), dma((ng, NX - 1)), dma((ng, NZ - 1)), dma((ng, NZ - 1)),
        dma((ng, NX - 1)), dma((ng, NX - 1)),
    ]
    square = jax.ShapeDtypeStruct((WIDTH, WIDTH), f32)
    rows = jax.ShapeDtypeStruct((ROWS, WIDTH), bf16)
    gain_row = gain.reshape(1, WIDTH)
    parts = pl.pallas_call(
        functools.partial(kernel, bits),
        out_shape=(rows, rows) + tuple(jax.ShapeDtypeStruct((n, HALF), bf16) for n in size),
        in_specs=[vmem] * 7 + [smem, vmem],
        out_specs=(vmem,) * (2 + ng),
        scratch_shapes=scratch,
        compiler_params=pltpu.CompilerParams(
            collective_id=0, has_side_effects=True, vmem_limit_bytes=58 * 2**20
        ),
    )(
        inputs[0], gain_row, w_query, w_key, w_value, w_out,
        block_slots.reshape(1, ROWS), matchings, cotangent[0],
    )
    update, grad_inputs, gq, gk, gv, go, gg = pl.pallas_call(
        finish,
        out_shape=(rows, rows, square, square, square, square,
                   jax.ShapeDtypeStruct((1, WIDTH), f32)),
        in_specs=[vmem] * (6 + ng),
        out_specs=(vmem,) * 7,
    )(*parts, gain_row, w_query, w_key, w_value)
    return update[None], grad_inputs[None], gq, gk, gv, go, gg[0]


def solution(mesh):
    placed = (
        P("dp", "graph", None), P(), P(), P(), P(), P(), P("graph"), P(), P("dp", "graph", None),
    )
    return jax.shard_map(
        local,
        mesh=mesh,
        in_specs=placed,
        out_specs=(P("dp", "graph", None), P("dp", "graph", None), P(), P(), P(), P(), P()),
        check_vma=False,
    )
```

```python
import functools

import jax
import jax.numpy as jnp
from jax import lax
from jax.experimental import pallas as pl
from jax.experimental.pallas import tpu as pltpu
from jax.sharding import PartitionSpec as P

MESH = pl.DeviceIdType.MESH
SPAN = 256
WIDTH = 256
HEAD = 32
HALF = 128
QUART = 64
PIECES = 4
KEYS = 1280
CHUNKS = 5
ROUNDS = 4
ROWS = 512
NX = 32
NZ = 8
EPS = 1e-06
LOG2E = 1.4426950408889634
SCALE = HEAD ** (-0.5)
GROUPS = ((0, 1, 2), (3,))
EARLY = 2

f32 = jnp.float32
bf16 = jnp.bfloat16


def dot(a, b):
    return jnp.dot(a, b, preferred_element_type=f32)


def dot_nt(a, b):
    return lax.dot_general(a, b, (((1,), (1,)), ((), ())), preferred_element_type=f32)


def flipped(value, mask):
    out = value
    bit = 1
    while bit <= mask:
        if mask & bit:
            out = out + bit - 2 * bit * lax.rem(lax.div(value, bit), 2)
        bit *= 2
    return out


def fold(array, op):
    return op(array.reshape(array.shape[0] // 8, 8, array.shape[1]), axis=0)


def remote(src, dst, send, recv, to):
    return pltpu.make_async_remote_copy(
        src_ref=src, dst_ref=dst, send_sem=send, recv_sem=recv,
        device_id=to, device_id_type=MESH,
    )


def kernel(bits, *refs):
    (
        x_ref, gain_ref, wq_ref, wk_ref, wv_ref, wo_ref, slot_ref, match_ref, cot_ref,
        upd_ref, ginp_ref,
    ) = refs[:11]
    ng = len(GROUPS)
    a1 = refs[11 : 11 + ng]
    refs = refs[11 + ng :]
    (
        oht, slot_f, inv_s, normed, nf0, nf1, nf2, nf3, normed_t,
        keys, vals, keys_t, vals_t, cots_t, wkv, qm, gm,
        att_t, dq_t, dkv, exps, stack, mixer,
    ) = refs[:23]
    got = [refs[23 + 4 * p : 27 + 4 * p] for p in range(PIECES)]
    refs = refs[39:]
    gf, gw, r1, s2, r3 = [refs[ng * k : ng * k + ng] for k in range(5)]
    (
        ns_send, ns_recv, ds_send, ds_recv,
        s1_send, s1_recv, s3_send, s3_recv, t1_send, t1_recv, news_x, news_z,
    ) = refs[5 * ng :]

    gi = lax.axis_index("graph")
    dp = lax.axis_index("dp")
    spot = lax.rem(gi, 8) + 8 * lax.div(gi, 16)
    far = (nf0, nf1, nf2, nf3)
    partners = [(dp, flipped(gi, 1 << bit)) for bit in bits]
    x_peer = [(dp, flipped(gi, m % 8 + 16 * (m // 8))) for m in range(1, NX)]
    z_peer = [(flipped(dp, m // 2), flipped(gi, 8 * (m % 2))) for m in range(1, NZ)]

    barrier = pltpu.get_barrier_semaphore()
    x_step = [x_peer[m - 1] for m in (1, 2, 4, 8, 16)]
    z_step = [z_peer[m - 1] for m in (1, 2, 6)]
    for peer in x_step + z_step:
        pl.semaphore_signal(barrier, inc=1, device_id=peer, device_id_type=MESH)

    def tell(k):
        for step, news in ((x_step, news_x), (z_step, news_z)):
            if 1 <= k <= len(step):
                pl.semaphore_wait(news.at[k - 1], 1)
            if k < len(step):
                pl.semaphore_signal(
                    news.at[k], inc=1, device_id=step[k], device_id_type=MESH
                )

    hot_t = (
        lax.broadcasted_iota(jnp.int32, (ROWS, ROWS), 0) == slot_ref[...] - gi * ROWS
    ).astype(f32).astype(bf16)
    oht[...] = hot_t
    hot = hot_t.T
    sx = dot(hot, x_ref[...])
    slot_f[...] = sx
    inv = lax.rsqrt(jnp.mean(sx * sx, axis=-1, keepdims=True) + EPS)
    inv_s[...] = inv
    gain = gain_ref[...]
    nrm = (sx * inv * gain).astype(bf16)
    for b in range(2):
        normed[b] = nrm[b * SPAN : (b + 1) * SPAN]

    pl.semaphore_wait(barrier, 8)
    sends = []
    far_copies = []
    for r in range(ROUNDS):
        far_copies.append(
            remote(normed, far[r], ns_send.at[r], ns_recv.at[r], partners[r])
        )
    for copy in far_copies:
        copy.start()
        sends.append(copy)
    tell(0)

    mixer[...] = jnp.zeros_like(mixer)
    cs = dot(hot, cot_ref[...]).astype(bf16)
    cots_t[...] = cs.T
    wk_t = wk_ref[...].T
    wv_t = wv_ref[...].T
    for p in range(PIECES):
        part = slice(p * QUART, (p + 1) * QUART)
        wkv[p * HALF : p * HALF + QUART] = wk_t[part]
        wkv[p * HALF + QUART : (p + 1) * HALF] = wv_t[part]
    q_t = dot_nt(wq_ref[...].T, nrm).astype(bf16)
    g_t = dot_nt(wo_ref[...], cs).astype(bf16)
    head_of = lax.broadcasted_iota(jnp.int32, (HALF, SPAN), 0) // HEAD
    for g in range(2):
        for b in range(2):
            qs = q_t[g * HALF : (g + 1) * HALF, b * SPAN : (b + 1) * SPAN]
            gs = g_t[g * HALF : (g + 1) * HALF, b * SPAN : (b + 1) * SPAN]
            for hh in range(4):
                qm[b, 4 * g + hh] = jnp.where(head_of == hh, qs, jnp.zeros_like(qs))
                gm[b, 4 * g + hh] = jnp.where(head_of == hh, gs, jnp.zeros_like(gs))

    def add_keys(b, c, rows):
        span = pl.ds(c * SPAN, SPAN)
        k = dot(rows, wk_ref[...]).astype(bf16)
        v = dot(rows, wv_ref[...]).astype(bf16)
        for g in range(2):
            half = slice(g * HALF, (g + 1) * HALF)
            keys[b, g, span, :] = k[:, half]
            vals[b, g, span, :] = v[:, half]
        keys_t[b, :, span] = dot_nt(wk_t, rows).astype(bf16)
        vals_t[b, :, span] = dot_nt(wv_t, rows).astype(bf16)
        normed_t[b, :, span] = rows.T

    units = [(p, b, 2 * p + i) for p in range(PIECES) for b in range(2) for i in range(2)]
    top = {}
    total = {}
    out = {}
    scale_of = {}
    shift = {}
    delta = {}
    dq = {}

    def scores(u, c):
        p, b, h = units[u]
        span = pl.ds(c * SPAN, SPAN)
        s = dot(keys[b, p // 2, span, :], qm[b, h])
        exps[u, span, :] = s
        m = fold(s, jnp.max)
        top[u] = m if c == 0 else jnp.maximum(top[u], m)

    def softmax(u, c):
        p, b, h = units[u]
        span = pl.ds(c * SPAN, SPAN)
        if c == 0:
            shift[u] = jnp.max(top[u], axis=0, keepdims=True) * (SCALE * LOG2E)
        e = jnp.exp2(exps[u, span, :] * (SCALE * LOG2E) - shift[u])
        exps[u, span, :] = e
        t = fold(e, jnp.sum)
        total[u] = t if c == 0 else total[u] + t
        eb = e.astype(bf16)
        stack[(u // 2) % 2, span, pl.ds((2 + u % 2) * SPAN, SPAN)] = eb
        o = dot(vals_t[b, pl.ds(h * HEAD, HEAD), span], eb)
        out[u] = o if c == 0 else out[u] + o

    def middle(u):
        p, b, h = units[u]
        i = u % 2
        rinv = 1.0 / jnp.sum(total[u], axis=0, keepdims=True)
        o = out[u] * rinv
        att_t[pl.ds(h * HEAD, HEAD), pl.ds(b * SPAN, SPAN)] = o.astype(bf16)
        row = pl.ds((h % 4) * HEAD, HEAD)
        grad = gm[b, h, row, :].astype(f32)
        query = qm[b, h, row, :].astype(f32)
        delta[u] = jnp.sum(grad * o, axis=0, keepdims=True)
        scale_of[u] = rinv * SCALE
        half = (u // 2) % 2
        mixer[half, pl.ds(i * HEAD, HEAD), pl.ds(i * SPAN, SPAN)] = (
            query * scale_of[u]
        ).astype(bf16)
        mixer[half, pl.ds(QUART + i * HEAD, HEAD), pl.ds((2 + i) * SPAN, SPAN)] = (
            grad * rinv
        ).astype(bf16)

    def score_grad(u, c):
        p, b, h = units[u]
        span = pl.ds(c * SPAN, SPAN)
        dprob = dot(vals[b, p // 2, span, :], gm[b, h])
        ds = (exps[u, span, :] * (dprob - delta[u])).astype(bf16)
        stack[(u // 2) % 2, span, pl.ds((u % 2) * SPAN, SPAN)] = ds
        q = dot(keys_t[b, pl.ds(h * HEAD, HEAD), span], ds)
        dq[u] = q if c == 0 else dq[u] + q

    def close(u):
        p, b, h = units[u]
        dq_t[pl.ds(h * HEAD, HEAD), pl.ds(b * SPAN, SPAN)] = (dq[u] * scale_of[u]).astype(bf16)

    def key_grads(u, c):
        p, b, h = units[u]
        half = (u // 2) % 2
        dkv[p, c, b] = dot_nt(
            stack[half, pl.ds(c * SPAN, SPAN), :], mixer[half]
        ).astype(bf16)

    def weight_grads(k):
        for i, p in enumerate(GROUPS[k]):
            feats = pl.ds(p * QUART, QUART)
            kv = None
            for b in range(2):
                for c in range(CHUNKS):
                    part = dot(normed_t[b, :, c * SPAN : (c + 1) * SPAN], dkv[p, c, b])
                    kv = part if kv is None else kv + part
            gq = dot_nt(normed_t[0, :, 0:SPAN], dq_t[feats, 0:SPAN]) + dot_nt(
                normed_t[1, :, 0:SPAN], dq_t[feats, SPAN:ROWS]
            )
            go = dot_nt(cots_t[...], att_t[feats, :])
            both = jnp.concatenate([gq, go], axis=1)
            at = i * ROWS
            gf[k][at : at + WIDTH] = kv
            gf[k][at + WIDTH : at + ROWS] = both
            gw[k][at : at + WIDTH] = kv.astype(bf16)
            gw[k][at + WIDTH : at + ROWS] = both.astype(bf16)

    grads_far = {}

    def send_grads(p):
        grads_far[p] = [
            remote(
                dkv.at[p, r + 1], got[p][r], ds_send.at[p, r], ds_recv.at[p, r], partners[r]
            )
            for r in range(ROUNDS)
        ]
        for copy in grads_far[p]:
            copy.start()
        sends.extend(grads_far[p])

    flight = {}

    def start(name, k, copies):
        for copy in copies:
            copy.start()
        sends.extend(copies)
        flight[name, k] = copies

    def arrived(name, k):
        for copy in flight[name, k]:
            copy.wait_recv()

    def spread(k):
        n = len(GROUPS[k]) * ROWS // NX
        start("s1", k, [
            remote(
                gw[k].at[pl.ds(flipped(spot, m) * n, n)], r1[k].at[m - 1],
                s1_send.at[k, m - 1], s1_recv.at[k, m - 1], x_peer[m - 1],
            )
            for m in range(1, NX)
        ])

    def across(k):
        n = len(GROUPS[k]) * ROWS // NX
        arrived("s1", k)
        acc = gf[k][pl.ds(spot * n, n)]
        for m in range(1, NX):
            acc = acc + r1[k][m - 1].astype(f32)
        s2[k][...] = acc
        start("s3", k, [
            remote(
                s2[k], r3[k].at[m - 1],
                s3_send.at[k, m - 1], s3_recv.at[k, m - 1], z_peer[m - 1],
            )
            for m in range(1, NZ)
        ])

    def gather(k):
        n = len(GROUPS[k]) * ROWS // NX
        arrived("s3", k)
        mine = pl.ds(spot * n, n)
        level = [s2[k][...]] + [r3[k][m - 1] for m in range(1, NZ)]
        while len(level) > 1:
            level = [level[j] + level[j + 1] for j in range(0, len(level), 2)]
        a1[k][mine] = level[0].astype(bf16)
        start("t1", k, [
            remote(
                a1[k].at[mine], a1[k].at[mine],
                t1_send.at[k, m - 1], t1_recv.at[k, m - 1], x_peer[m - 1],
            )
            for m in range(1, NX)
        ])

    tell(1)
    for b in range(2):
        add_keys(b, 0, normed[b])
    for u in range(len(units)):
        for c in range(min(EARLY, 1)):
            scores(u, c)
    pairs = [
        [lax.rem(match_ref[r, 2 * gi + b], 2) for b in range(2)] for r in range(ROUNDS)
    ]
    for r in range(ROUNDS):
        if r == 1:
            tell(2)
        far_copies[r].wait_recv()
        for b in range(2):
            add_keys(b, r + 1, far[r][pairs[r][b]])
        if r + 1 < EARLY:
            for u in range(len(units)):
                scores(u, r + 1)

    tell(3)
    hooks = {
        2: [lambda: tell(4)],
        4: [lambda: tell(5), lambda: send_grads(0)],
        8: [lambda: send_grads(1)],
        12: [lambda: weight_grads(0), lambda: spread(0), lambda: send_grads(2)],
    }
    last = len(units) - 1
    for c in range(EARLY, CHUNKS):
        scores(0, c)
    for u in range(len(units)):
        for c in range(CHUNKS):
            if u < last and c >= EARLY:
                scores(u + 1, c)
            softmax(u, c)
        middle(u)
        for c in range(CHUNKS):
            score_grad(u, c)
            if u % 2 == 0 and u >= 2:
                key_grads(u - 1, c)
        close(u)
        for hook in hooks.get(u, []):
            hook()
    for c in range(CHUNKS):
        key_grads(last, c)
    weight_grads(1)
    spread(1)
    send_grads(3)

    upd = dot(att_t[...].T, wo_ref[...]).astype(bf16)
    upd_ref[...] = dot(oht[...], upd).astype(bf16)
    across(0)
    ng_q = dot_nt(dq_t[...].T, wq_ref[...])
    def key_total(p, b):
        t = dkv[p, 0, b].astype(f32)
        for r in range(ROUNDS):
            t = t + got[p][r][pairs[r][b]].astype(f32)
        return t.astype(bf16)

    across(1)
    for p in range(PIECES):
        for copy in grads_far[p]:
            copy.wait_recv()
    outs = []
    for b in range(2):
        sums = jnp.concatenate([key_total(p, b) for p in range(PIECES)], axis=1)
        rows = slice(b * SPAN, (b + 1) * SPAN)
        ngrad = ng_q[rows] + dot(sums, wkv[...])
        scaled = ngrad * gain
        x = slot_f[rows]
        iv = inv_s[rows]
        mean = jnp.mean(x * scaled, axis=-1, keepdims=True)
        outs.append((iv * scaled - x * (iv * iv * iv) * mean).astype(bf16))
    ginp_ref[...] = dot(oht[...], jnp.concatenate(outs, axis=0)).astype(bf16)
    gather(0)
    gather(1)
    for k in range(ng):
        arrived("t1", k)
    for copy in sends:
        copy.wait_send()


def finish(*refs):
    ng = len(GROUPS)
    upd, ginp = refs[:2]
    sums = refs[2 : 2 + ng]
    gain_ref, wq_ref, wk_ref, wv_ref = refs[2 + ng : 6 + ng]
    upd_ref, ginp_ref, gq_ref, gk_ref, gv_ref, go_ref, gg_ref = refs[6 + ng :]
    upd_ref[...] = upd[...]
    ginp_ref[...] = ginp[...]
    kv = {}
    qo = {}
    for k, group in enumerate(GROUPS):
        for i, p in enumerate(group):
            at = i * ROWS
            kv[p] = sums[k][at : at + WIDTH].astype(f32)
            qo[p] = sums[k][at + WIDTH : at + ROWS].astype(f32)
    first, second = slice(0, QUART), slice(QUART, HALF)

    def joined(parts, half):
        return jnp.concatenate([parts[p][:, half] for p in range(PIECES)], axis=1)

    gk, gv, gq = joined(kv, first), joined(kv, second), joined(qo, first)
    gq_ref[...] = gq
    gk_ref[...] = gk
    gv_ref[...] = gv
    go_ref[...] = joined(qo, second).T
    prod = (
        gq * wq_ref[...].astype(f32) + gk * wk_ref[...].astype(f32)
        + gv * wv_ref[...].astype(f32)
    )
    gg_ref[...] = jnp.sum(prod.T, axis=0, keepdims=True) / gain_ref[...]


def local(inputs, gain, w_query, w_key, w_value, w_out, block_slots, matchings, cotangent):
    nbits = lax.axis_size("graph").bit_length() - 1
    rounds = matchings.shape[0]
    bits = tuple(turn * nbits // rounds for turn in range(rounds))
    vmem = pl.BlockSpec(memory_space=pltpu.VMEM)
    smem = pl.BlockSpec(memory_space=pltpu.SMEM)
    dma = pltpu.SemaphoreType.DMA
    ng = len(GROUPS)
    size = [len(group) * ROWS for group in GROUPS]
    far = pltpu.VMEM((2, SPAN, WIDTH), bf16)
    got = pltpu.VMEM((2, SPAN, HALF), bf16)
    units = 4 * PIECES
    scratch = [
        pltpu.VMEM((ROWS, ROWS), bf16),
        pltpu.VMEM((ROWS, WIDTH), f32),
        pltpu.VMEM((ROWS, 1), f32),
        far, far, far, far, far,
        pltpu.VMEM((2, WIDTH, KEYS), bf16),
        pltpu.VMEM((2, 2, KEYS, HALF), bf16),
        pltpu.VMEM((2, 2, KEYS, HALF), bf16),
        pltpu.VMEM((2, WIDTH, KEYS), bf16),
        pltpu.VMEM((2, WIDTH, KEYS), bf16),
        pltpu.VMEM((WIDTH, ROWS), bf16),
        pltpu.VMEM((ROWS, WIDTH), bf16),
        pltpu.VMEM((2, 8, HALF, SPAN), bf16),
        pltpu.VMEM((2, 8, HALF, SPAN), bf16),
        pltpu.VMEM((WIDTH, ROWS), bf16),
        pltpu.VMEM((WIDTH, ROWS), bf16),
        pltpu.VMEM((PIECES, CHUNKS, 2, SPAN, HALF), bf16),
        pltpu.VMEM((units, KEYS, SPAN), f32),
        pltpu.VMEM((2, KEYS, 4 * SPAN), bf16),
        pltpu.VMEM((2, HALF, 4 * SPAN), bf16),
    ]
    scratch += [got] * (PIECES * ROUNDS)
    scratch += [pltpu.VMEM((n, HALF), f32) for n in size]
    scratch += [pltpu.VMEM((n, HALF), bf16) for n in size]
    scratch += [pltpu.VMEM((NX - 1, n // NX, HALF), bf16) for n in size]
    scratch += [pltpu.VMEM((n // NX, HALF), f32) for n in size]
    scratch += [pltpu.VMEM((NZ - 1, n // NX, HALF), f32) for n in size]
    scratch += [
        dma((ROUNDS,)), dma((ROUNDS,)), dma((PIECES, ROUNDS)), dma((PIECES, ROUNDS)),
        dma((ng, NX - 1)), dma((ng, NX - 1)), dma((ng, NZ - 1)), dma((ng, NZ - 1)),
        dma((ng, NX - 1)), dma((ng, NX - 1)),
        pltpu.SemaphoreType.REGULAR((5,)), pltpu.SemaphoreType.REGULAR((3,)),
    ]
    square = jax.ShapeDtypeStruct((WIDTH, WIDTH), f32)
    rows = jax.ShapeDtypeStruct((ROWS, WIDTH), bf16)
    gain_row = gain.reshape(1, WIDTH)
    parts = pl.pallas_call(
        functools.partial(kernel, bits),
        out_shape=(rows, rows) + tuple(jax.ShapeDtypeStruct((n, HALF), bf16) for n in size),
        in_specs=[vmem] * 7 + [smem, vmem],
        out_specs=(vmem,) * (2 + ng),
        scratch_shapes=scratch,
        compiler_params=pltpu.CompilerParams(
            collective_id=0, has_side_effects=True, vmem_limit_bytes=58 * 2**20
        ),
    )(
        inputs[0], gain_row, w_query, w_key, w_value, w_out,
        block_slots.reshape(1, ROWS), matchings, cotangent[0],
    )
    update, grad_inputs, gq, gk, gv, go, gg = pl.pallas_call(
        finish,
        out_shape=(rows, rows, square, square, square, square,
                   jax.ShapeDtypeStruct((1, WIDTH), f32)),
        in_specs=[vmem] * (6 + ng),
        out_specs=(vmem,) * 7,
    )(*parts, gain_row, w_query, w_key, w_value)
    return update[None], grad_inputs[None], gq, gk, gv, go, gg[0]


def solution(mesh):
    placed = (
        P("dp", "graph", None), P(), P(), P(), P(), P(), P("graph"), P(), P("dp", "graph", None),
    )
    return jax.shard_map(
        local,
        mesh=mesh,
        in_specs=placed,
        out_specs=(P("dp", "graph", None), P("dp", "graph", None), P(), P(), P(), P(), P()),
        check_vma=False,
    )
```

```python
import functools

import jax
import jax.numpy as jnp
from jax import lax
from jax.experimental import pallas as pl
from jax.experimental.pallas import tpu as pltpu
from jax.sharding import PartitionSpec as P

MESH = pl.DeviceIdType.MESH
SPAN = 256
WIDTH = 256
HEAD = 32
HALF = 128
QUART = 64
PIECES = 4
KEYS = 1280
CHUNKS = 5
ROUNDS = 4
ROWS = 512
NX = 32
NZ = 8
EPS = 1e-06
LOG2E = 1.4426950408889634
SCALE = HEAD ** (-0.5)
GROUPS = ((0, 1, 2), (3,))
EARLY = 2
RING4 = (0, 1, 2, 1)
X_ORDER = sorted(range(1, NX), key=lambda m: -RING4[m // 2 % 4] - RING4[m // 8])
Z_ORDER = sorted(range(1, NZ), key=lambda m: -2 * RING4[m // 2] - m % 2)

f32 = jnp.float32
bf16 = jnp.bfloat16


def dot(a, b):
    return jnp.dot(a, b, preferred_element_type=f32)


def dot_nt(a, b):
    return lax.dot_general(a, b, (((1,), (1,)), ((), ())), preferred_element_type=f32)


def flipped(value, mask):
    out = value
    bit = 1
    while bit <= mask:
        if mask & bit:
            out = out + bit - 2 * bit * lax.rem(lax.div(value, bit), 2)
        bit *= 2
    return out


def fold(array, op):
    return op(array.reshape(array.shape[0] // 8, 8, array.shape[1]), axis=0)


def remote(src, dst, send, recv, to):
    return pltpu.make_async_remote_copy(
        src_ref=src, dst_ref=dst, send_sem=send, recv_sem=recv,
        device_id=to, device_id_type=MESH,
    )


def kernel(bits, *refs):
    (
        x_ref, gain_ref, wq_ref, wk_ref, wv_ref, wo_ref, slot_ref, match_ref, cot_ref,
        upd_ref, ginp_ref,
    ) = refs[:11]
    ng = len(GROUPS)
    a1 = refs[11 : 11 + ng]
    refs = refs[11 + ng :]
    (
        oht, slot_f, inv_s, normed, nf0, nf1, nf2, nf3, normed_t,
        keys, vals, keys_t, vals_t, cots_t, wkv, qm, gm,
        att_t, dq_t, dkv, exps, stack, mixer,
    ) = refs[:23]
    got = [refs[23 + 4 * p : 27 + 4 * p] for p in range(PIECES)]
    refs = refs[39:]
    gf, gw, r1, s2, r3 = [refs[ng * k : ng * k + ng] for k in range(5)]
    (
        ns_send, ns_recv, ds_send, ds_recv,
        s1_send, s1_recv, s3_send, s3_recv, t1_send, t1_recv, news_x, news_z,
    ) = refs[5 * ng :]

    gi = lax.axis_index("graph")
    dp = lax.axis_index("dp")
    spot = lax.rem(gi, 8) + 8 * lax.div(gi, 16)
    far = (nf0, nf1, nf2, nf3)
    partners = [(dp, flipped(gi, 1 << bit)) for bit in bits]
    x_peer = [(dp, flipped(gi, m % 8 + 16 * (m // 8))) for m in range(1, NX)]
    z_peer = [(flipped(dp, m // 2), flipped(gi, 8 * (m % 2))) for m in range(1, NZ)]

    barrier = pltpu.get_barrier_semaphore()
    x_step = [x_peer[m - 1] for m in (1, 2, 4, 8, 16)]
    z_step = [z_peer[m - 1] for m in (1, 2, 6)]
    for peer in x_step + z_step:
        pl.semaphore_signal(barrier, inc=1, device_id=peer, device_id_type=MESH)

    def tell(k):
        for step, news in ((x_step, news_x), (z_step, news_z)):
            if 1 <= k <= len(step):
                pl.semaphore_wait(news.at[k - 1], 1)
            if k < len(step):
                pl.semaphore_signal(
                    news.at[k], inc=1, device_id=step[k], device_id_type=MESH
                )

    hot_t = (
        lax.broadcasted_iota(jnp.int32, (ROWS, ROWS), 0) == slot_ref[...] - gi * ROWS
    ).astype(f32).astype(bf16)
    oht[...] = hot_t
    hot = hot_t.T
    sx = dot(hot, x_ref[...])
    slot_f[...] = sx
    inv = lax.rsqrt(jnp.mean(sx * sx, axis=-1, keepdims=True) + EPS)
    inv_s[...] = inv
    gain = gain_ref[...]
    nrm = (sx * inv * gain).astype(bf16)
    for b in range(2):
        normed[b] = nrm[b * SPAN : (b + 1) * SPAN]

    pl.semaphore_wait(barrier, 8)
    sends = []
    far_copies = []
    for r in range(ROUNDS):
        far_copies.append(
            remote(normed, far[r], ns_send.at[r], ns_recv.at[r], partners[r])
        )
    for copy in far_copies:
        copy.start()
        sends.append(copy)
    tell(0)

    mixer[...] = jnp.zeros_like(mixer)
    cs = dot(hot, cot_ref[...]).astype(bf16)
    cots_t[...] = cs.T
    wk_t = wk_ref[...].T
    wv_t = wv_ref[...].T
    for p in range(PIECES):
        part = slice(p * QUART, (p + 1) * QUART)
        wkv[p * HALF : p * HALF + QUART] = wk_t[part]
        wkv[p * HALF + QUART : (p + 1) * HALF] = wv_t[part]
    q_t = dot_nt(wq_ref[...].T, nrm).astype(bf16)
    g_t = dot_nt(wo_ref[...], cs).astype(bf16)
    head_of = lax.broadcasted_iota(jnp.int32, (HALF, SPAN), 0) // HEAD
    for g in range(2):
        for b in range(2):
            qs = q_t[g * HALF : (g + 1) * HALF, b * SPAN : (b + 1) * SPAN]
            gs = g_t[g * HALF : (g + 1) * HALF, b * SPAN : (b + 1) * SPAN]
            for hh in range(4):
                qm[b, 4 * g + hh] = jnp.where(head_of == hh, qs, jnp.zeros_like(qs))
                gm[b, 4 * g + hh] = jnp.where(head_of == hh, gs, jnp.zeros_like(gs))

    def add_keys(b, c, rows):
        span = pl.ds(c * SPAN, SPAN)
        k = dot(rows, wk_ref[...]).astype(bf16)
        v = dot(rows, wv_ref[...]).astype(bf16)
        for g in range(2):
            half = slice(g * HALF, (g + 1) * HALF)
            keys[b, g, span, :] = k[:, half]
            vals[b, g, span, :] = v[:, half]
        keys_t[b, :, span] = dot_nt(wk_t, rows).astype(bf16)
        vals_t[b, :, span] = dot_nt(wv_t, rows).astype(bf16)
        normed_t[b, :, span] = rows.T

    units = [(p, b, 2 * p + i) for p in range(PIECES) for b in range(2) for i in range(2)]
    top = {}
    total = {}
    out = {}
    scale_of = {}
    shift = {}
    delta = {}
    dq = {}

    def scores(u, c):
        p, b, h = units[u]
        span = pl.ds(c * SPAN, SPAN)
        s = dot(keys[b, p // 2, span, :], qm[b, h])
        exps[u, span, :] = s
        m = fold(s, jnp.max)
        top[u] = m if c == 0 else jnp.maximum(top[u], m)

    def softmax(u, c):
        p, b, h = units[u]
        span = pl.ds(c * SPAN, SPAN)
        if c == 0:
            shift[u] = jnp.max(top[u], axis=0, keepdims=True) * (SCALE * LOG2E)
        e = jnp.exp2(exps[u, span, :] * (SCALE * LOG2E) - shift[u])
        exps[u, span, :] = e
        t = fold(e, jnp.sum)
        total[u] = t if c == 0 else total[u] + t
        eb = e.astype(bf16)
        stack[(u // 2) % 2, span, pl.ds((2 + u % 2) * SPAN, SPAN)] = eb
        o = dot(vals_t[b, pl.ds(h * HEAD, HEAD), span], eb)
        out[u] = o if c == 0 else out[u] + o

    def middle(u):
        p, b, h = units[u]
        i = u % 2
        rinv = 1.0 / jnp.sum(total[u], axis=0, keepdims=True)
        o = out[u] * rinv
        att_t[pl.ds(h * HEAD, HEAD), pl.ds(b * SPAN, SPAN)] = o.astype(bf16)
        row = pl.ds((h % 4) * HEAD, HEAD)
        grad = gm[b, h, row, :].astype(f32)
        query = qm[b, h, row, :].astype(f32)
        delta[u] = jnp.sum(grad * o, axis=0, keepdims=True)
        scale_of[u] = rinv * SCALE
        half = (u // 2) % 2
        mixer[half, pl.ds(i * HEAD, HEAD), pl.ds(i * SPAN, SPAN)] = (
            query * scale_of[u]
        ).astype(bf16)
        mixer[half, pl.ds(QUART + i * HEAD, HEAD), pl.ds((2 + i) * SPAN, SPAN)] = (
            grad * rinv
        ).astype(bf16)

    def score_grad(u, c):
        p, b, h = units[u]
        span = pl.ds(c * SPAN, SPAN)
        dprob = dot(vals[b, p // 2, span, :], gm[b, h])
        ds = (exps[u, span, :] * (dprob - delta[u])).astype(bf16)
        stack[(u // 2) % 2, span, pl.ds((u % 2) * SPAN, SPAN)] = ds
        q = dot(keys_t[b, pl.ds(h * HEAD, HEAD), span], ds)
        dq[u] = q if c == 0 else dq[u] + q

    def close(u):
        p, b, h = units[u]
        dq_t[pl.ds(h * HEAD, HEAD), pl.ds(b * SPAN, SPAN)] = (dq[u] * scale_of[u]).astype(bf16)

    def key_grads(u, c):
        p, b, h = units[u]
        half = (u // 2) % 2
        dkv[p, c, b] = dot_nt(
            stack[half, pl.ds(c * SPAN, SPAN), :], mixer[half]
        ).astype(bf16)

    def weight_grads(k):
        for i, p in enumerate(GROUPS[k]):
            feats = pl.ds(p * QUART, QUART)
            kv = None
            for b in range(2):
                for c in range(CHUNKS):
                    part = dot(normed_t[b, :, c * SPAN : (c + 1) * SPAN], dkv[p, c, b])
                    kv = part if kv is None else kv + part
            gq = dot_nt(normed_t[0, :, 0:SPAN], dq_t[feats, 0:SPAN]) + dot_nt(
                normed_t[1, :, 0:SPAN], dq_t[feats, SPAN:ROWS]
            )
            go = dot_nt(cots_t[...], att_t[feats, :])
            both = jnp.concatenate([gq, go], axis=1)
            at = i * ROWS
            gf[k][at : at + WIDTH] = kv
            gf[k][at + WIDTH : at + ROWS] = both
            gw[k][at : at + WIDTH] = kv.astype(bf16)
            gw[k][at + WIDTH : at + ROWS] = both.astype(bf16)

    grads_far = {}

    def send_grads(p):
        grads_far[p] = [
            remote(
                dkv.at[p, r + 1], got[p][r], ds_send.at[p, r], ds_recv.at[p, r], partners[r]
            )
            for r in range(ROUNDS)
        ]
        for copy in grads_far[p]:
            copy.start()
        sends.extend(grads_far[p])

    flight = {}

    def start(name, k, copies):
        for copy in copies:
            copy.start()
        sends.extend(copies)
        flight[name, k] = copies

    def arrived(name, k):
        for copy in flight[name, k]:
            copy.wait_recv()

    def spread(k):
        n = len(GROUPS[k]) * ROWS // NX
        start("s1", k, [
            remote(
                gw[k].at[pl.ds(flipped(spot, m) * n, n)], r1[k].at[m - 1],
                s1_send.at[k, m - 1], s1_recv.at[k, m - 1], x_peer[m - 1],
            )
            for m in X_ORDER
        ])

    def across(k):
        n = len(GROUPS[k]) * ROWS // NX
        arrived("s1", k)
        acc = gf[k][pl.ds(spot * n, n)]
        for m in range(1, NX):
            acc = acc + r1[k][m - 1].astype(f32)
        s2[k][...] = acc
        start("s3", k, [
            remote(
                s2[k], r3[k].at[m - 1],
                s3_send.at[k, m - 1], s3_recv.at[k, m - 1], z_peer[m - 1],
            )
            for m in Z_ORDER
        ])

    def gather(k):
        n = len(GROUPS[k]) * ROWS // NX
        arrived("s3", k)
        mine = pl.ds(spot * n, n)
        level = [s2[k][...]] + [r3[k][m - 1] for m in range(1, NZ)]
        while len(level) > 1:
            level = [level[j] + level[j + 1] for j in range(0, len(level), 2)]
        a1[k][mine] = level[0].astype(bf16)
        start("t1", k, [
            remote(
                a1[k].at[mine], a1[k].at[mine],
                t1_send.at[k, m - 1], t1_recv.at[k, m - 1], x_peer[m - 1],
            )
            for m in X_ORDER
        ])

    tell(1)
    for b in range(2):
        add_keys(b, 0, normed[b])
    for u in range(len(units)):
        for c in range(min(EARLY, 1)):
            scores(u, c)
    pairs = [
        [lax.rem(match_ref[r, 2 * gi + b], 2) for b in range(2)] for r in range(ROUNDS)
    ]
    for r in range(ROUNDS):
        if r == 1:
            tell(2)
        far_copies[r].wait_recv()
        for b in range(2):
            add_keys(b, r + 1, far[r][pairs[r][b]])
        if r + 1 < EARLY:
            for u in range(len(units)):
                scores(u, r + 1)

    tell(3)
    hooks = {
        2: [lambda: tell(4)],
        4: [lambda: tell(5), lambda: send_grads(0)],
        8: [lambda: send_grads(1)],
        12: [lambda: weight_grads(0), lambda: spread(0), lambda: send_grads(2)],
    }
    last = len(units) - 1
    for c in range(EARLY, CHUNKS):
        scores(0, c)
    for u in range(len(units)):
        for c in range(CHUNKS):
            if u < last and c >= EARLY:
                scores(u + 1, c)
            softmax(u, c)
        middle(u)
        for c in range(CHUNKS):
            score_grad(u, c)
            if u % 2 == 0 and u >= 2:
                key_grads(u - 1, c)
        close(u)
        for hook in hooks.get(u, []):
            hook()
    for c in range(CHUNKS):
        key_grads(last, c)
    weight_grads(1)
    spread(1)
    send_grads(3)

    upd = dot(att_t[...].T, wo_ref[...]).astype(bf16)
    upd_ref[...] = dot(oht[...], upd).astype(bf16)
    across(0)
    ng_q = dot_nt(dq_t[...].T, wq_ref[...])
    def key_total(p, b):
        t = dkv[p, 0, b].astype(f32)
        for r in range(ROUNDS):
            t = t + got[p][r][pairs[r][b]].astype(f32)
        return t.astype(bf16)

    across(1)
    gather(0)
    for p in range(PIECES):
        for copy in grads_far[p]:
            copy.wait_recv()
    outs = []
    for b in range(2):
        sums = jnp.concatenate([key_total(p, b) for p in range(PIECES)], axis=1)
        rows = slice(b * SPAN, (b + 1) * SPAN)
        ngrad = ng_q[rows] + dot(sums, wkv[...])
        scaled = ngrad * gain
        x = slot_f[rows]
        iv = inv_s[rows]
        mean = jnp.mean(x * scaled, axis=-1, keepdims=True)
        outs.append((iv * scaled - x * (iv * iv * iv) * mean).astype(bf16))
    ginp_ref[...] = dot(oht[...], jnp.concatenate(outs, axis=0)).astype(bf16)
    gather(1)
    for k in range(ng):
        arrived("t1", k)
    for copy in sends:
        copy.wait_send()


def finish(*refs):
    ng = len(GROUPS)
    upd, ginp = refs[:2]
    sums = refs[2 : 2 + ng]
    gain_ref, wq_ref, wk_ref, wv_ref = refs[2 + ng : 6 + ng]
    upd_ref, ginp_ref, gq_ref, gk_ref, gv_ref, go_ref, gg_ref = refs[6 + ng :]
    upd_ref[...] = upd[...]
    ginp_ref[...] = ginp[...]
    kv = {}
    qo = {}
    for k, group in enumerate(GROUPS):
        for i, p in enumerate(group):
            at = i * ROWS
            kv[p] = sums[k][at : at + WIDTH].astype(f32)
            qo[p] = sums[k][at + WIDTH : at + ROWS].astype(f32)
    first, second = slice(0, QUART), slice(QUART, HALF)

    def joined(parts, half):
        return jnp.concatenate([parts[p][:, half] for p in range(PIECES)], axis=1)

    gk, gv, gq = joined(kv, first), joined(kv, second), joined(qo, first)
    gq_ref[...] = gq
    gk_ref[...] = gk
    gv_ref[...] = gv
    go_ref[...] = joined(qo, second).T
    prod = (
        gq * wq_ref[...].astype(f32) + gk * wk_ref[...].astype(f32)
        + gv * wv_ref[...].astype(f32)
    )
    gg_ref[...] = jnp.sum(prod.T, axis=0, keepdims=True) / gain_ref[...]


def local(inputs, gain, w_query, w_key, w_value, w_out, block_slots, matchings, cotangent):
    nbits = lax.axis_size("graph").bit_length() - 1
    rounds = matchings.shape[0]
    bits = tuple(turn * nbits // rounds for turn in range(rounds))
    vmem = pl.BlockSpec(memory_space=pltpu.VMEM)
    smem = pl.BlockSpec(memory_space=pltpu.SMEM)
    dma = pltpu.SemaphoreType.DMA
    ng = len(GROUPS)
    size = [len(group) * ROWS for group in GROUPS]
    far = pltpu.VMEM((2, SPAN, WIDTH), bf16)
    got = pltpu.VMEM((2, SPAN, HALF), bf16)
    units = 4 * PIECES
    scratch = [
        pltpu.VMEM((ROWS, ROWS), bf16),
        pltpu.VMEM((ROWS, WIDTH), f32),
        pltpu.VMEM((ROWS, 1), f32),
        far, far, far, far, far,
        pltpu.VMEM((2, WIDTH, KEYS), bf16),
        pltpu.VMEM((2, 2, KEYS, HALF), bf16),
        pltpu.VMEM((2, 2, KEYS, HALF), bf16),
        pltpu.VMEM((2, WIDTH, KEYS), bf16),
        pltpu.VMEM((2, WIDTH, KEYS), bf16),
        pltpu.VMEM((WIDTH, ROWS), bf16),
        pltpu.VMEM((ROWS, WIDTH), bf16),
        pltpu.VMEM((2, 8, HALF, SPAN), bf16),
        pltpu.VMEM((2, 8, HALF, SPAN), bf16),
        pltpu.VMEM((WIDTH, ROWS), bf16),
        pltpu.VMEM((WIDTH, ROWS), bf16),
        pltpu.VMEM((PIECES, CHUNKS, 2, SPAN, HALF), bf16),
        pltpu.VMEM((units, KEYS, SPAN), f32),
        pltpu.VMEM((2, KEYS, 4 * SPAN), bf16),
        pltpu.VMEM((2, HALF, 4 * SPAN), bf16),
    ]
    scratch += [got] * (PIECES * ROUNDS)
    scratch += [pltpu.VMEM((n, HALF), f32) for n in size]
    scratch += [pltpu.VMEM((n, HALF), bf16) for n in size]
    scratch += [pltpu.VMEM((NX - 1, n // NX, HALF), bf16) for n in size]
    scratch += [pltpu.VMEM((n // NX, HALF), f32) for n in size]
    scratch += [pltpu.VMEM((NZ - 1, n // NX, HALF), f32) for n in size]
    scratch += [
        dma((ROUNDS,)), dma((ROUNDS,)), dma((PIECES, ROUNDS)), dma((PIECES, ROUNDS)),
        dma((ng, NX - 1)), dma((ng, NX - 1)), dma((ng, NZ - 1)), dma((ng, NZ - 1)),
        dma((ng, NX - 1)), dma((ng, NX - 1)),
        pltpu.SemaphoreType.REGULAR((5,)), pltpu.SemaphoreType.REGULAR((3,)),
    ]
    square = jax.ShapeDtypeStruct((WIDTH, WIDTH), f32)
    rows = jax.ShapeDtypeStruct((ROWS, WIDTH), bf16)
    gain_row = gain.reshape(1, WIDTH)
    parts = pl.pallas_call(
        functools.partial(kernel, bits),
        out_shape=(rows, rows) + tuple(jax.ShapeDtypeStruct((n, HALF), bf16) for n in size),
        in_specs=[vmem] * 7 + [smem, vmem],
        out_specs=(vmem,) * (2 + ng),
        scratch_shapes=scratch,
        compiler_params=pltpu.CompilerParams(
            collective_id=0, has_side_effects=True, vmem_limit_bytes=58 * 2**20
        ),
    )(
        inputs[0], gain_row, w_query, w_key, w_value, w_out,
        block_slots.reshape(1, ROWS), matchings, cotangent[0],
    )
    update, grad_inputs, gq, gk, gv, go, gg = pl.pallas_call(
        finish,
        out_shape=(rows, rows, square, square, square, square,
                   jax.ShapeDtypeStruct((1, WIDTH), f32)),
        in_specs=[vmem] * (6 + ng),
        out_specs=(vmem,) * 7,
    )(*parts, gain_row, w_query, w_key, w_value)
    return update[None], grad_inputs[None], gq, gk, gv, go, gg[0]


def solution(mesh):
    placed = (
        P("dp", "graph", None), P(), P(), P(), P(), P(), P("graph"), P(), P("dp", "graph", None),
    )
    return jax.shard_map(
        local,
        mesh=mesh,
        in_specs=placed,
        out_specs=(P("dp", "graph", None), P("dp", "graph", None), P(), P(), P(), P(), P()),
        check_vma=False,
    )
```

```python
import functools

import jax
import jax.numpy as jnp
from jax import lax
from jax.experimental import pallas as pl
from jax.experimental.pallas import tpu as pltpu
from jax.sharding import PartitionSpec as P

MESH = pl.DeviceIdType.MESH
SPAN = 256
WIDTH = 256
HEAD = 32
HALF = 128
QUART = 64
PIECES = 4
KEYS = 1280
CHUNKS = 5
ROUNDS = 4
ROWS = 512
NX = 32
NZ = 8
EPS = 1e-06
LOG2E = 1.4426950408889634
SCALE = HEAD ** (-0.5)
GROUPS = ((0, 1, 2), (3,))
EARLY = 2
RING4 = (0, 1, 2, 1)
X_ORDER = sorted(range(1, NX), key=lambda m: -RING4[m // 2 % 4] - RING4[m // 8])
Z_ORDER = sorted(range(1, NZ), key=lambda m: -2 * RING4[m // 2] - m % 2)

f32 = jnp.float32
bf16 = jnp.bfloat16


def dot(a, b):
    return jnp.dot(a, b, preferred_element_type=f32)


def dot_nt(a, b):
    return lax.dot_general(a, b, (((1,), (1,)), ((), ())), preferred_element_type=f32)


def flipped(value, mask):
    out = value
    bit = 1
    while bit <= mask:
        if mask & bit:
            out = out + bit - 2 * bit * lax.rem(lax.div(value, bit), 2)
        bit *= 2
    return out


def fold(array, op):
    return op(array.reshape(array.shape[0] // 8, 8, array.shape[1]), axis=0)


def remote(src, dst, send, recv, to):
    return pltpu.make_async_remote_copy(
        src_ref=src, dst_ref=dst, send_sem=send, recv_sem=recv,
        device_id=to, device_id_type=MESH,
    )


def kernel(bits, *refs):
    (
        x_hbm, gain_ref, wq_hbm, wk_hbm, wv_hbm, wo_hbm, slot_ref, match_ref, cot_hbm,
        upd_ref, ginp_ref,
    ) = refs[:11]
    ng = len(GROUPS)
    a1 = refs[11 : 11 + ng]
    refs = refs[11 + ng :]
    (
        oht, slot_f, inv_s, normed, nf0, nf1, nf2, nf3, normed_t,
        keys, vals, keys_t, vals_t, cots_t, wkv, qm, gm,
        att_t, dq_t, dkv, exps, stack, mixer,
    ) = refs[:23]
    got = [refs[23 + 4 * p : 27 + 4 * p] for p in range(PIECES)]
    refs = refs[39:]
    gf, gw, r1, s2, r3 = [refs[ng * k : ng * k + ng] for k in range(5)]
    (
        ns_send, ns_recv, ds_send, ds_recv,
        s1_send, s1_recv, s3_send, s3_recv, t1_send, t1_recv, news_x, news_z,
        x_ref, cot_ref, wq_ref, wk_ref, wv_ref, wo_ref, in_sem,
    ) = refs[5 * ng :]

    gi = lax.axis_index("graph")
    dp = lax.axis_index("dp")
    spot = lax.rem(gi, 8) + 8 * lax.div(gi, 16)
    far = (nf0, nf1, nf2, nf3)
    partners = [(dp, flipped(gi, 1 << bit)) for bit in bits]
    x_peer = [(dp, flipped(gi, m % 8 + 16 * (m // 8))) for m in range(1, NX)]
    z_peer = [(flipped(dp, m // 2), flipped(gi, 8 * (m % 2))) for m in range(1, NZ)]

    barrier = pltpu.get_barrier_semaphore()
    x_step = [x_peer[m - 1] for m in (1, 2, 4, 8, 16)]
    z_step = [z_peer[m - 1] for m in (1, 2, 6)]
    for peer in x_step + z_step:
        pl.semaphore_signal(barrier, inc=1, device_id=peer, device_id_type=MESH)

    def tell(k):
        for step, news in ((x_step, news_x), (z_step, news_z)):
            if 1 <= k <= len(step):
                pl.semaphore_wait(news.at[k - 1], 1)
            if k < len(step):
                pl.semaphore_signal(
                    news.at[k], inc=1, device_id=step[k], device_id_type=MESH
                )

    loads = [
        pltpu.make_async_copy(src, dst, in_sem.at[j])
        for j, (src, dst) in enumerate((
            (x_hbm, x_ref), (cot_hbm, cot_ref), (wk_hbm, wk_ref), (wv_hbm, wv_ref),
            (wq_hbm, wq_ref), (wo_hbm, wo_ref),
        ))
    ]
    for load in loads:
        load.start()

    hot_t = (
        lax.broadcasted_iota(jnp.int32, (ROWS, ROWS), 0) == slot_ref[...] - gi * ROWS
    ).astype(f32).astype(bf16)
    oht[...] = hot_t
    hot = hot_t.T
    loads[0].wait()
    sx = dot(hot, x_ref[...])
    slot_f[...] = sx
    inv = lax.rsqrt(jnp.mean(sx * sx, axis=-1, keepdims=True) + EPS)
    inv_s[...] = inv
    gain = gain_ref[...]
    nrm = (sx * inv * gain).astype(bf16)
    for b in range(2):
        normed[b] = nrm[b * SPAN : (b + 1) * SPAN]

    pl.semaphore_wait(barrier, 8)
    sends = []
    far_copies = []
    for r in range(ROUNDS):
        far_copies.append(
            remote(normed, far[r], ns_send.at[r], ns_recv.at[r], partners[r])
        )
    for copy in far_copies:
        copy.start()
        sends.append(copy)
    tell(0)

    mixer[...] = jnp.zeros_like(mixer)
    for load in loads[1:]:
        load.wait()
    cs = dot(hot, cot_ref[...]).astype(bf16)
    cots_t[...] = cs.T
    wk_t = wk_ref[...].T
    wv_t = wv_ref[...].T
    for p in range(PIECES):
        part = slice(p * QUART, (p + 1) * QUART)
        wkv[p * HALF : p * HALF + QUART] = wk_t[part]
        wkv[p * HALF + QUART : (p + 1) * HALF] = wv_t[part]
    q_t = dot_nt(wq_ref[...].T, nrm).astype(bf16)
    g_t = dot_nt(wo_ref[...], cs).astype(bf16)
    head_of = lax.broadcasted_iota(jnp.int32, (HALF, SPAN), 0) // HEAD
    for g in range(2):
        for b in range(2):
            qs = q_t[g * HALF : (g + 1) * HALF, b * SPAN : (b + 1) * SPAN]
            gs = g_t[g * HALF : (g + 1) * HALF, b * SPAN : (b + 1) * SPAN]
            for hh in range(4):
                qm[b, 4 * g + hh] = jnp.where(head_of == hh, qs, jnp.zeros_like(qs))
                gm[b, 4 * g + hh] = jnp.where(head_of == hh, gs, jnp.zeros_like(gs))

    def add_keys(b, c, rows):
        span = pl.ds(c * SPAN, SPAN)
        k = dot(rows, wk_ref[...]).astype(bf16)
        v = dot(rows, wv_ref[...]).astype(bf16)
        for g in range(2):
            half = slice(g * HALF, (g + 1) * HALF)
            keys[b, g, span, :] = k[:, half]
            vals[b, g, span, :] = v[:, half]
        keys_t[b, :, span] = dot_nt(wk_t, rows).astype(bf16)
        vals_t[b, :, span] = dot_nt(wv_t, rows).astype(bf16)
        normed_t[b, :, span] = rows.T

    units = [(p, b, 2 * p + i) for p in range(PIECES) for b in range(2) for i in range(2)]
    top = {}
    total = {}
    out = {}
    scale_of = {}
    shift = {}
    delta = {}
    dq = {}

    def scores(u, c):
        p, b, h = units[u]
        span = pl.ds(c * SPAN, SPAN)
        s = dot(keys[b, p // 2, span, :], qm[b, h])
        exps[u, span, :] = s
        m = fold(s, jnp.max)
        top[u] = m if c == 0 else jnp.maximum(top[u], m)

    def softmax(u, c):
        p, b, h = units[u]
        span = pl.ds(c * SPAN, SPAN)
        if c == 0:
            shift[u] = jnp.max(top[u], axis=0, keepdims=True) * (SCALE * LOG2E)
        e = jnp.exp2(exps[u, span, :] * (SCALE * LOG2E) - shift[u])
        exps[u, span, :] = e
        t = fold(e, jnp.sum)
        total[u] = t if c == 0 else total[u] + t
        eb = e.astype(bf16)
        stack[(u // 2) % 2, span, pl.ds((2 + u % 2) * SPAN, SPAN)] = eb
        o = dot(vals_t[b, pl.ds(h * HEAD, HEAD), span], eb)
        out[u] = o if c == 0 else out[u] + o

    def middle(u):
        p, b, h = units[u]
        i = u % 2
        rinv = 1.0 / jnp.sum(total[u], axis=0, keepdims=True)
        o = out[u] * rinv
        att_t[pl.ds(h * HEAD, HEAD), pl.ds(b * SPAN, SPAN)] = o.astype(bf16)
        row = pl.ds((h % 4) * HEAD, HEAD)
        grad = gm[b, h, row, :].astype(f32)
        query = qm[b, h, row, :].astype(f32)
        delta[u] = jnp.sum(grad * o, axis=0, keepdims=True)
        scale_of[u] = rinv * SCALE
        half = (u // 2) % 2
        mixer[half, pl.ds(i * HEAD, HEAD), pl.ds(i * SPAN, SPAN)] = (
            query * scale_of[u]
        ).astype(bf16)
        mixer[half, pl.ds(QUART + i * HEAD, HEAD), pl.ds((2 + i) * SPAN, SPAN)] = (
            grad * rinv
        ).astype(bf16)

    def score_grad(u, c):
        p, b, h = units[u]
        span = pl.ds(c * SPAN, SPAN)
        dprob = dot(vals[b, p // 2, span, :], gm[b, h])
        ds = (exps[u, span, :] * (dprob - delta[u])).astype(bf16)
        stack[(u // 2) % 2, span, pl.ds((u % 2) * SPAN, SPAN)] = ds
        q = dot(keys_t[b, pl.ds(h * HEAD, HEAD), span], ds)
        dq[u] = q if c == 0 else dq[u] + q

    def close(u):
        p, b, h = units[u]
        dq_t[pl.ds(h * HEAD, HEAD), pl.ds(b * SPAN, SPAN)] = (dq[u] * scale_of[u]).astype(bf16)

    def key_grads(u, c):
        p, b, h = units[u]
        half = (u // 2) % 2
        dkv[p, c, b] = dot_nt(
            stack[half, pl.ds(c * SPAN, SPAN), :], mixer[half]
        ).astype(bf16)

    def weight_grads(k):
        for i, p in enumerate(GROUPS[k]):
            feats = pl.ds(p * QUART, QUART)
            kv = None
            for b in range(2):
                for c in range(CHUNKS):
                    part = dot(normed_t[b, :, c * SPAN : (c + 1) * SPAN], dkv[p, c, b])
                    kv = part if kv is None else kv + part
            gq = dot_nt(normed_t[0, :, 0:SPAN], dq_t[feats, 0:SPAN]) + dot_nt(
                normed_t[1, :, 0:SPAN], dq_t[feats, SPAN:ROWS]
            )
            go = dot_nt(cots_t[...], att_t[feats, :])
            both = jnp.concatenate([gq, go], axis=1)
            at = i * ROWS
            gf[k][at : at + WIDTH] = kv
            gf[k][at + WIDTH : at + ROWS] = both
            gw[k][at : at + WIDTH] = kv.astype(bf16)
            gw[k][at + WIDTH : at + ROWS] = both.astype(bf16)

    grads_far = {}

    def send_grads(p):
        grads_far[p] = [
            remote(
                dkv.at[p, r + 1], got[p][r], ds_send.at[p, r], ds_recv.at[p, r], partners[r]
            )
            for r in range(ROUNDS)
        ]
        for copy in grads_far[p]:
            copy.start()
        sends.extend(grads_far[p])

    flight = {}

    def start(name, k, copies):
        for copy in copies:
            copy.start()
        sends.extend(copies)
        flight[name, k] = copies

    def arrived(name, k):
        for copy in flight[name, k]:
            copy.wait_recv()

    def spread(k):
        n = len(GROUPS[k]) * ROWS // NX
        start("s1", k, [
            remote(
                gw[k].at[pl.ds(flipped(spot, m) * n, n)], r1[k].at[m - 1],
                s1_send.at[k, m - 1], s1_recv.at[k, m - 1], x_peer[m - 1],
            )
            for m in X_ORDER
        ])

    def across(k):
        n = len(GROUPS[k]) * ROWS // NX
        arrived("s1", k)
        acc = gf[k][pl.ds(spot * n, n)]
        for m in range(1, NX):
            acc = acc + r1[k][m - 1].astype(f32)
        s2[k][...] = acc
        start("s3", k, [
            remote(
                s2[k], r3[k].at[m - 1],
                s3_send.at[k, m - 1], s3_recv.at[k, m - 1], z_peer[m - 1],
            )
            for m in Z_ORDER
        ])

    def gather(k):
        n = len(GROUPS[k]) * ROWS // NX
        arrived("s3", k)
        mine = pl.ds(spot * n, n)
        level = [s2[k][...]] + [r3[k][m - 1] for m in range(1, NZ)]
        while len(level) > 1:
            level = [level[j] + level[j + 1] for j in range(0, len(level), 2)]
        a1[k][mine] = level[0].astype(bf16)
        start("t1", k, [
            remote(
                a1[k].at[mine], a1[k].at[mine],
                t1_send.at[k, m - 1], t1_recv.at[k, m - 1], x_peer[m - 1],
            )
            for m in X_ORDER
        ])

    tell(1)
    for b in range(2):
        add_keys(b, 0, normed[b])
    for u in range(len(units)):
        for c in range(min(EARLY, 1)):
            scores(u, c)
    pairs = [
        [lax.rem(match_ref[r, 2 * gi + b], 2) for b in range(2)] for r in range(ROUNDS)
    ]
    for r in range(ROUNDS):
        if r == 1:
            tell(2)
        far_copies[r].wait_recv()
        for b in range(2):
            add_keys(b, r + 1, far[r][pairs[r][b]])
        if r + 1 < EARLY:
            for u in range(len(units)):
                scores(u, r + 1)

    tell(3)
    hooks = {
        2: [lambda: tell(4)],
        4: [lambda: tell(5), lambda: send_grads(0)],
        8: [lambda: send_grads(1)],
        12: [lambda: weight_grads(0), lambda: spread(0), lambda: send_grads(2)],
    }
    last = len(units) - 1
    for c in range(EARLY, CHUNKS):
        scores(0, c)
    for u in range(len(units)):
        for c in range(CHUNKS):
            if u < last and c >= EARLY:
                scores(u + 1, c)
            softmax(u, c)
        middle(u)
        for c in range(CHUNKS):
            score_grad(u, c)
            if u % 2 == 0 and u >= 2:
                key_grads(u - 1, c)
        close(u)
        for hook in hooks.get(u, []):
            hook()
    for c in range(CHUNKS):
        key_grads(last, c)
    weight_grads(1)
    spread(1)
    send_grads(3)

    upd = dot(att_t[...].T, wo_ref[...]).astype(bf16)
    upd_ref[...] = dot(oht[...], upd).astype(bf16)
    across(0)
    ng_q = dot_nt(dq_t[...].T, wq_ref[...])
    def key_total(p, b):
        t = dkv[p, 0, b].astype(f32)
        for r in range(ROUNDS):
            t = t + got[p][r][pairs[r][b]].astype(f32)
        return t.astype(bf16)

    across(1)
    gather(0)
    for p in range(PIECES):
        for copy in grads_far[p]:
            copy.wait_recv()
    outs = []
    for b in range(2):
        sums = jnp.concatenate([key_total(p, b) for p in range(PIECES)], axis=1)
        rows = slice(b * SPAN, (b + 1) * SPAN)
        ngrad = ng_q[rows] + dot(sums, wkv[...])
        scaled = ngrad * gain
        x = slot_f[rows]
        iv = inv_s[rows]
        mean = jnp.mean(x * scaled, axis=-1, keepdims=True)
        outs.append((iv * scaled - x * (iv * iv * iv) * mean).astype(bf16))
    ginp_ref[...] = dot(oht[...], jnp.concatenate(outs, axis=0)).astype(bf16)
    gather(1)
    for k in range(ng):
        arrived("t1", k)
    for copy in sends:
        copy.wait_send()


def finish(*refs):
    ng = len(GROUPS)
    upd, ginp = refs[:2]
    sums = refs[2 : 2 + ng]
    gain_ref, wq_ref, wk_ref, wv_ref = refs[2 + ng : 6 + ng]
    upd_ref, ginp_ref, gq_ref, gk_ref, gv_ref, go_ref, gg_ref = refs[6 + ng :]
    upd_ref[...] = upd[...]
    ginp_ref[...] = ginp[...]
    kv = {}
    qo = {}
    for k, group in enumerate(GROUPS):
        for i, p in enumerate(group):
            at = i * ROWS
            kv[p] = sums[k][at : at + WIDTH].astype(f32)
            qo[p] = sums[k][at + WIDTH : at + ROWS].astype(f32)
    first, second = slice(0, QUART), slice(QUART, HALF)

    def joined(parts, half):
        return jnp.concatenate([parts[p][:, half] for p in range(PIECES)], axis=1)

    gk, gv, gq = joined(kv, first), joined(kv, second), joined(qo, first)
    gq_ref[...] = gq
    gk_ref[...] = gk
    gv_ref[...] = gv
    go_ref[...] = joined(qo, second).T
    prod = (
        gq * wq_ref[...].astype(f32) + gk * wk_ref[...].astype(f32)
        + gv * wv_ref[...].astype(f32)
    )
    gg_ref[...] = jnp.sum(prod.T, axis=0, keepdims=True) / gain_ref[...]


def local(inputs, gain, w_query, w_key, w_value, w_out, block_slots, matchings, cotangent):
    nbits = lax.axis_size("graph").bit_length() - 1
    rounds = matchings.shape[0]
    bits = tuple(turn * nbits // rounds for turn in range(rounds))
    vmem = pl.BlockSpec(memory_space=pltpu.VMEM)
    smem = pl.BlockSpec(memory_space=pltpu.SMEM)
    whole = pl.BlockSpec(memory_space=pl.ANY)
    dma = pltpu.SemaphoreType.DMA
    ng = len(GROUPS)
    size = [len(group) * ROWS for group in GROUPS]
    far = pltpu.VMEM((2, SPAN, WIDTH), bf16)
    got = pltpu.VMEM((2, SPAN, HALF), bf16)
    units = 4 * PIECES
    scratch = [
        pltpu.VMEM((ROWS, ROWS), bf16),
        pltpu.VMEM((ROWS, WIDTH), f32),
        pltpu.VMEM((ROWS, 1), f32),
        far, far, far, far, far,
        pltpu.VMEM((2, WIDTH, KEYS), bf16),
        pltpu.VMEM((2, 2, KEYS, HALF), bf16),
        pltpu.VMEM((2, 2, KEYS, HALF), bf16),
        pltpu.VMEM((2, WIDTH, KEYS), bf16),
        pltpu.VMEM((2, WIDTH, KEYS), bf16),
        pltpu.VMEM((WIDTH, ROWS), bf16),
        pltpu.VMEM((ROWS, WIDTH), bf16),
        pltpu.VMEM((2, 8, HALF, SPAN), bf16),
        pltpu.VMEM((2, 8, HALF, SPAN), bf16),
        pltpu.VMEM((WIDTH, ROWS), bf16),
        pltpu.VMEM((WIDTH, ROWS), bf16),
        pltpu.VMEM((PIECES, CHUNKS, 2, SPAN, HALF), bf16),
        pltpu.VMEM((units, KEYS, SPAN), f32),
        pltpu.VMEM((2, KEYS, 4 * SPAN), bf16),
        pltpu.VMEM((2, HALF, 4 * SPAN), bf16),
    ]
    scratch += [got] * (PIECES * ROUNDS)
    scratch += [pltpu.VMEM((n, HALF), f32) for n in size]
    scratch += [pltpu.VMEM((n, HALF), bf16) for n in size]
    scratch += [pltpu.VMEM((NX - 1, n // NX, HALF), bf16) for n in size]
    scratch += [pltpu.VMEM((n // NX, HALF), f32) for n in size]
    scratch += [pltpu.VMEM((NZ - 1, n // NX, HALF), f32) for n in size]
    scratch += [
        dma((ROUNDS,)), dma((ROUNDS,)), dma((PIECES, ROUNDS)), dma((PIECES, ROUNDS)),
        dma((ng, NX - 1)), dma((ng, NX - 1)), dma((ng, NZ - 1)), dma((ng, NZ - 1)),
        dma((ng, NX - 1)), dma((ng, NX - 1)),
        pltpu.SemaphoreType.REGULAR((5,)), pltpu.SemaphoreType.REGULAR((3,)),
        pltpu.VMEM((ROWS, WIDTH), bf16), pltpu.VMEM((ROWS, WIDTH), bf16),
        pltpu.VMEM((WIDTH, WIDTH), bf16), pltpu.VMEM((WIDTH, WIDTH), bf16),
        pltpu.VMEM((WIDTH, WIDTH), bf16), pltpu.VMEM((WIDTH, WIDTH), bf16),
        dma((6,)),
    ]
    square = jax.ShapeDtypeStruct((WIDTH, WIDTH), f32)
    rows = jax.ShapeDtypeStruct((ROWS, WIDTH), bf16)
    gain_row = gain.reshape(1, WIDTH)
    parts = pl.pallas_call(
        functools.partial(kernel, bits),
        out_shape=(rows, rows) + tuple(jax.ShapeDtypeStruct((n, HALF), bf16) for n in size),
        in_specs=[whole, vmem, whole, whole, whole, whole, vmem, smem, whole],
        out_specs=(vmem,) * (2 + ng),
        scratch_shapes=scratch,
        compiler_params=pltpu.CompilerParams(
            collective_id=0, has_side_effects=True, vmem_limit_bytes=58 * 2**20
        ),
    )(
        inputs[0], gain_row, w_query, w_key, w_value, w_out,
        block_slots.reshape(1, ROWS), matchings, cotangent[0],
    )
    update, grad_inputs, gq, gk, gv, go, gg = pl.pallas_call(
        finish,
        out_shape=(rows, rows, square, square, square, square,
                   jax.ShapeDtypeStruct((1, WIDTH), f32)),
        in_specs=[vmem] * (6 + ng),
        out_specs=(vmem,) * 7,
    )(*parts, gain_row, w_query, w_key, w_value)
    return update[None], grad_inputs[None], gq, gk, gv, go, gg[0]


def solution(mesh):
    placed = (
        P("dp", "graph", None), P(), P(), P(), P(), P(), P("graph"), P(), P("dp", "graph", None),
    )
    return jax.shard_map(
        local,
        mesh=mesh,
        in_specs=placed,
        out_specs=(P("dp", "graph", None), P("dp", "graph", None), P(), P(), P(), P(), P()),
        check_vma=False,
    )
```
